32 devices in a mesh: design: 2 (over y), gx: 4 (over z), gy: 4 (over x, core).
Axes of the slice: x: 2, y: 2, z: 4, core: 2. Of those that a mesh axis runs over, the one named last changes fastest.
Arguments:
- e_field: float32 [6, 8, 64, 1024], P('design', None, 'gx', 'gy'), parts along dimension 0, may hold values from -6 to 6
- h_field: float32 [6, 8, 64, 1024], P('design', None, 'gx', 'gy'), parts along dimension 0, may hold values from -6 to 6
- pol_now: float32 [6, 8, 64, 1024], P('design', None, 'gx', 'gy'), parts along dimension 0, may hold values from -3 to 3
- pol_old: float32 [6, 8, 64, 1024], P('design', None, 'gx', 'gy'), parts along dimension 0, may hold values from -3 to 3
- eps_inf: float32 [16, 64, 1024], P('design', 'gx', 'gy'), parts along dimension 0, may hold values from 1 to 4
- materials: int32 [16, 64, 1024], P('design', 'gx', 'gy'), parts along dimension 0, may hold values from 0 to 15
- surface: int32 [4, 64, 1024], P('design', 'gx', 'gy'), parts along dimension 0, may hold values 0 or 1
- poles: float32 [3, 16], replicated, may hold values from 0.2 to 0.9
- directions: float32 [4096, 2], replicated, may hold values from -0.7 to 0.7
Outputs:
- e_final: float32 [6, 8, 64, 1024], P('design', None, 'gx', 'gy'), parts along dimension 0
- h_final: float32 [6, 8, 64, 1024], P('design', None, 'gx', 'gy'), parts along dimension 0
- far_field: float32 [4096, 32], P(('gx', 'gy'), 'design'), parts along dimension 1
The draws below stay inside these ranges and needn't reach their ends.
There are 2 independent parts, one for each index of `design`. The reference program is written for one: setup_inputs(seed, part) draws one part's arguments, and reference() takes and returns one part's arrays. A program takes and returns all parts, laid end to end along the dimension named above; an argument that names none is the same for every part. Nothing has to cross between parts.
All inputs are finite; a program needn't handle non-finite values. No bound on the sum of `surface` on one device may be relied on, other than what follows from the above.
Results may differ from the reference program's by a relative error of at most 0.0003.
Values sent between devices are 32-bit elements; how exact they have to be, the bound alone decides.
No kernel may reach another device: no remote copies, remote signals or barrier semaphores. Data moves between devices by JAX's collectives and lax.ppermute only.
A program may use at most 64 MiB of HBM per device.

```python
import math
import jax
import jax.numpy as jnp
from jax import lax

NZ = 8
NMAT = 16
NDIR = 4096
STEPS = 2
NX = 64
NY = 1024


def set_ends(drawn, rng, low, high):
    dims = drawn.shape
    spot = [jax.random.randint(jax.random.fold_in(rng, axis), (), 0, dims[axis]) for axis in range(len(dims))]
    drawn = drawn.at[tuple(spot)].set(low)
    longest = dims.index(max(dims))
    spot[longest] = (spot[longest] + 1) % dims[longest]
    return drawn.at[tuple(spot)].set(high)


def shard_levels(key, shape, split, smallest, largest):
    gain, own = 1.0, jax.random.fold_in(key, 6)
    for axis_at, parts in split:
        draws = jnp.exp(jax.random.uniform(jax.random.fold_in(own, axis_at), (parts,), jnp.float32, smallest / len(split), largest / len(split)))
        gain = gain * jnp.repeat(draws, shape[axis_at] // parts).reshape([-1 if axis == axis_at else 1 for axis in range(len(shape))])
    return gain


def bell_draw(own_key, dims, scale, reach, cuts=(), held_as=jnp.bfloat16):
    drawn = scale * jax.random.normal(own_key, dims, jnp.float32)
    if cuts:
        drawn = drawn * shard_levels(own_key, dims, cuts, -0.22, 0.18)
    return jnp.clip(drawn, -reach, reach).astype(held_as)


def setup_inputs(seed: int = 0, part: int = 0) -> dict:
    streams_of = jax.random.split(jax.random.key(seed), 10)
    own_keys = jax.random.split(jax.random.fold_in(streams_of[9], part), 10)
    e_field = bell_draw(own_keys[0], (3, NZ, NX, NY), 1.0, 6.0, ((2, 4), (3, 4)), jnp.float32)
    h_field = bell_draw(own_keys[1], (3, NZ, NX, NY), 1.0, 6.0, ((2, 4), (3, 4)), jnp.float32)
    pol_now = bell_draw(own_keys[2], (3, NZ, NX, NY), 0.5, 3.0, ((2, 4), (3, 4)), jnp.float32)
    pol_old = bell_draw(own_keys[3], (3, NZ, NX, NY), 0.5, 3.0, ((2, 4), (3, 4)), jnp.float32)
    eps_inf = jnp.clip(1.0 + 3.0 * jax.random.uniform(own_keys[4], (NZ, NX, NY), jnp.float32) ** shard_levels(own_keys[4], (NZ, NX, NY), ((1, 4), (2, 4)), -0.2, 0.2), 1.0, 4.0)
    materials = set_ends(jax.random.randint(own_keys[5], (NZ, NX, NY), 0, NMAT), jax.random.fold_in(own_keys[5], 1), 0, NMAT - 1).astype(jnp.int32)
    surface = set_ends((jax.random.randint(own_keys[6], (2, NX, NY), 0, 2) < 1).astype(jnp.int32), jax.random.fold_in(own_keys[6], 1), 0, 1)
    poles = jnp.clip(jax.random.uniform(streams_of[7], (3, NMAT), jnp.float32, 0.2, 0.9), 0.2, 0.9)
    directions = jnp.clip(jax.random.uniform(streams_of[8], (NDIR, 2), jnp.float32, -0.7, 0.7), -0.7, 0.7)
    return dict(e_field=e_field, h_field=h_field, pol_now=pol_now, pol_old=pol_old, eps_inf=eps_inf, materials=materials, surface=surface, poles=poles, directions=directions)


COURANT = 0.5
WAVE = 0.3
OMEGA = 0.25

def pole_table(poles, materials):
    omega_dt = poles[0]
    gamma_dt = poles[1]
    strength = poles[2]
    denominator = 1.0 + 0.5 * gamma_dt
    table_a = (2.0 - omega_dt * omega_dt) / denominator
    table_b = -(1.0 - 0.5 * gamma_dt) / denominator
    table_c = strength * omega_dt * omega_dt / denominator
    coef_a = jnp.zeros(materials.shape, poles.dtype)
    coef_b = jnp.zeros(materials.shape, poles.dtype)
    coef_c = jnp.zeros(materials.shape, poles.dtype)
    for number in range(poles.shape[1]):
        selected = materials == number
        coef_a = jnp.where(selected, table_a[number], coef_a)
        coef_b = jnp.where(selected, table_b[number], coef_b)
        coef_c = jnp.where(selected, table_c[number], coef_c)
    return (coef_a, coef_b, coef_c)

def curl_e(field, next_x, next_y):
    along_x = jnp.concatenate([field[:, :, 1:, :], next_x[:, :, None, :]], axis=2)
    along_y = jnp.concatenate([field[:, :, :, 1:], next_y[:, :, :, None]], axis=3)
    along_z = jnp.concatenate([field[:, 1:], jnp.zeros_like(field[:, :1])], axis=1)
    return jnp.stack([along_y[2] - field[2] - (along_z[1] - field[1]), along_z[0] - field[0] - (along_x[2] - field[2]), along_x[1] - field[1] - (along_y[0] - field[0])])

def curl_h(field, prev_x, prev_y):
    along_x = jnp.concatenate([prev_x[:, :, None, :], field[:, :, :-1, :]], axis=2)
    along_y = jnp.concatenate([prev_y[:, :, :, None], field[:, :, :, :-1]], axis=3)
    along_z = jnp.concatenate([jnp.zeros_like(field[:, :1]), field[:, :-1]], axis=1)
    return jnp.stack([field[2] - along_y[2] - (field[1] - along_z[1]), field[0] - along_z[0] - (field[2] - along_x[2]), field[1] - along_x[1] - (field[0] - along_y[0])])

def surface_plane(e_now, h_now, surface):
    rows = []
    for layer, level in ((0, 0), (1, e_now.shape[1] - 1)):
        weight = surface[layer].astype(e_now.dtype)
        rows = rows + [e_now[0, level] * weight, e_now[1, level] * weight, h_now[0, level] * weight, h_now[1, level] * weight]
    return jnp.stack(rows)

def project(items, chosen, x_coords, y_coords, scale):
    count = chosen.shape[0]
    width_x = x_coords.shape[0]
    width_y = y_coords.shape[0]
    angle_y = WAVE * chosen[:, 1:2] * y_coords[None, :]
    table_y = jnp.concatenate([jnp.cos(angle_y), jnp.sin(angle_y)], axis=0)
    real_sum = jnp.zeros((8, count), chosen.dtype)
    imag_sum = jnp.zeros((8, count), chosen.dtype)
    for plane, number in items:
        partial_rows = jnp.dot(plane.reshape(8 * width_x, width_y), table_y.T, precision=lax.Precision.HIGHEST)
        partial_rows = partial_rows.reshape(8, width_x, 2, count)
        part_cos = partial_rows[:, :, 0]
        part_sin = partial_rows[:, :, 1]
        angle_x = WAVE * chosen[:, 0:1] * x_coords[None, :] - OMEGA * number
        cos_x = jnp.cos(angle_x).T[None]
        sin_x = jnp.sin(angle_x).T[None]
        real_sum = real_sum + lax.optimization_barrier(jnp.sum(cos_x * part_cos - sin_x * part_sin, axis=1))
        imag_sum = imag_sum + lax.optimization_barrier(jnp.sum(sin_x * part_cos + cos_x * part_sin, axis=1))
    return jnp.concatenate([real_sum.T, imag_sum.T], axis=1) * scale

def reference(e_field, h_field, pol_now, pol_old, eps_inf, materials, surface, poles, directions):
    coef_a, coef_b, coef_c = pole_table(poles, materials)
    zero_x = jnp.zeros((3, NZ, NY), e_field.dtype)
    zero_y = jnp.zeros((3, NZ, NX), e_field.dtype)
    e_now, h_now, keep_now, keep_old = (e_field, h_field, pol_now, pol_old)
    items = []
    for number in range(1, STEPS + 1):
        h_now = h_now - COURANT * curl_e(e_now, zero_x, zero_y)
        keep_next = coef_a * keep_now + coef_b * keep_old + coef_c * e_now
        e_now = e_now + (COURANT * curl_h(h_now, zero_x, zero_y) - (keep_next - keep_now)) / eps_inf
        keep_old, keep_now = (keep_now, keep_next)
        items.append((surface_plane(e_now, h_now, surface), number))
    x_coords = jnp.arange(NX).astype(e_field.dtype)
    y_coords = jnp.arange(NY).astype(e_field.dtype)
    far_field = project(items, directions, x_coords, y_coords, 1.0 / math.sqrt(NX * NY))
    return (e_now, h_now, far_field)
```

```python
from functools import partial
import math

import jax
import jax.numpy as jnp
from jax import lax
from jax.experimental import pallas as pl
from jax.experimental.pallas import tpu as pltpu
from jax.sharding import PartitionSpec as P

COURANT = 0.5
WAVE = 0.3
OMEGA = 0.25
LANES = 128
ITEMS = 10
VMEM = pltpu.CompilerParams(vmem_limit_bytes=24 * 1024 * 1024)


def lane_index(shape):
    return lax.broadcasted_iota(jnp.int32, shape, len(shape) - 1)


def row_index(shape):
    return lax.broadcasted_iota(jnp.int32, shape, 0)


def sincos(angle):
    turns = jnp.round(angle * (0.5 / math.pi))
    rest = angle - turns * 6.28125
    rest = rest - turns * 0.0019350051879882812
    rest = rest - turns * 3.0199159819567e-07
    half = 0.5 * rest
    sq = half * half
    sin_half = 1.0 / 6227020800.0
    for term in (-1.0 / 39916800.0, 1.0 / 362880.0, -1.0 / 5040.0, 1.0 / 120.0, -1.0 / 6.0, 1.0):
        sin_half = sin_half * sq + term
    sin_half = sin_half * half
    cos_half = -1.0 / 87178291200.0
    for term in (1.0 / 479001600.0, -1.0 / 3628800.0, 1.0 / 40320.0, -1.0 / 720.0, 1.0 / 24.0, -0.5, 1.0):
        cos_half = cos_half * sq + term
    return 2.0 * sin_half * cos_half, 1.0 - 2.0 * sin_half * sin_half


def prepare_body(e_ref, h_ref, p_ref, q_ref, eps_ref, mat_ref, poles_ref, one_ref, two_ref, d_ref, g_ref, k_ref, table_ref):
    levels, rows, width = eps_ref.shape
    last = width - LANES
    table_ref[0:3, 0 : poles_ref.shape[1]] = poles_ref[...]
    omega_dt, gamma_dt, strength = (table_ref[i : i + 1, :] for i in range(3))
    denominator = 1.0 + 0.5 * gamma_dt
    tile = (rows, LANES)
    table_a = jnp.broadcast_to((2.0 - omega_dt * omega_dt) / denominator, tile)
    table_b = jnp.broadcast_to(-(1.0 - 0.5 * gamma_dt) / denominator, tile)
    table_c = jnp.broadcast_to(strength * omega_dt * omega_dt / denominator, tile)
    lane = lane_index(tile)
    even = lax.rem(lax.axis_index("gy"), 2) == 0
    for z in range(levels):
        up = jnp.zeros(tile, jnp.float32)
        down = jnp.zeros(tile, jnp.float32)
        for start in range(0, width, LANES):
            cut = slice(start, start + LANES)
            number = mat_ref[z, :, cut]
            a = jnp.take_along_axis(table_a, number, axis=1)
            b = jnp.take_along_axis(table_b, number, axis=1)
            c = jnp.take_along_axis(table_c, number, axis=1)
            inv = 1.0 / eps_ref[z, :, cut]
            half = COURANT * inv
            k_ref[0, z, :, cut] = half
            k_ref[1, z, :, cut] = 1.0 - c * inv
            items = [e_ref[i, z, :, cut] for i in range(3)] + [h_ref[i, z, :, cut] for i in range(3)]
            for i in range(3):
                now, old = p_ref[i, z, :, cut], q_ref[i, z, :, cut]
                new = a * now + b * old + c * items[i]
                local = items[i] - (new - now) * inv
                d_ref[i, z, :, cut] = local
                g_ref[i, z, :, cut] = ((a * new - new) + b * now) * inv
                items.append(local)
            items.append(half)
            for k, item in enumerate(items):
                if start == 0:
                    moved = pltpu.roll(item, 2 * k, 1) if k else item
                    down = jnp.where((lane >= 2 * k) & (lane < 2 * k + 2), moved, down)
                if start == last:
                    moved = pltpu.roll(item, LANES - 2 * k, 1) if k else item
                    up = jnp.where((lane >= LANES - 2 - 2 * k) & (lane < LANES - 2 * k), moved, up)
        one_ref[z] = jnp.where(even, up, down)
        two_ref[z] = jnp.where(even, down, up)


def prepare(e_field, h_field, pol_now, pol_old, eps_inf, materials, poles):
    levels, rows, width = eps_inf.shape
    message = jax.ShapeDtypeStruct((levels, rows, LANES), jnp.float32)
    field = jax.ShapeDtypeStruct(e_field.shape, jnp.float32)
    pair = jax.ShapeDtypeStruct((2, levels, rows, width), jnp.float32)
    return pl.pallas_call(
        prepare_body,
        out_shape=(message, message, field, field, pair),
        scratch_shapes=[pltpu.VMEM((8, LANES), jnp.float32)],
        compiler_params=VMEM,
        name="prepare",
    )(e_field, h_field, pol_now, pol_old, eps_inf, materials, poles)


def read_wide(own_ref, index, z, messages, item):
    before, after = messages
    lane = lane_index(before[z].shape)
    shift = 2 * item
    late = pltpu.roll(after[z], LANES - shift, 1) if item else after[z]
    early = pltpu.roll(before[z], shift, 1) if item else before[z]
    halo = jnp.where(lane < 2, late, jnp.where(lane >= LANES - 2, early, 0.0))
    return jnp.concatenate([own_ref[index, z], halo], axis=1)


def y_messages(one_ref, two_ref):
    place = lax.axis_index("gy")
    count = lax.axis_size("gy")
    even = lax.rem(place, 2) == 0
    before, after = [], []
    for z in range(one_ref.shape[0]):
        one, two = one_ref[z], two_ref[z]
        before.append(jnp.where(place > 0, jnp.where(even, two, one), 0.0))
        after.append(jnp.where(place < count - 1, jnp.where(even, one, two), 0.0))
    return before, after


def ahead_y(v):
    return pltpu.roll(v, v.shape[1] - 1, 1)


def behind_y(v):
    return pltpu.roll(v, 1, 1)


def ahead_x(v, row):
    at = row_index(v.shape)
    return jnp.where(at == v.shape[0] - 1, row, pltpu.roll(v, v.shape[0] - 1, 0))


def behind_x(v, row):
    at = row_index(v.shape)
    return jnp.where(at == 0, row, pltpu.roll(v, 1, 0))


def magnetic(e_here, e_above, h_here, row_y, row_z, keep):
    ex, ey, ez = e_here
    hx, hy, hz = h_here
    up_x, up_y = e_above
    hx = hx - COURANT * ((ahead_y(ez) - ez) - (up_y - ey))
    hy = hy - COURANT * ((up_x - ex) - (ahead_x(ez, row_z) - ez))
    hz = hz - COURANT * ((ahead_x(ey, row_y) - ey) - (ahead_y(ex) - ex))
    return [jnp.where(keep, v, 0.0) for v in (hx, hy, hz)]


def curl_back(h_here, h_below, row_y, row_z):
    hx, hy, hz = h_here
    low_x, low_y = h_below
    return (
        (hz - behind_y(hz)) - (hy - low_y),
        (hx - low_x) - (hz - behind_x(hz, row_z)),
        (hy - behind_x(hy, row_y)) - (hx - behind_y(hx)),
    )


def kept_lanes(shape, width):
    return (lane_index(shape) < width + LANES // 2) | (lax.axis_index("gy") > 0)


def first_body(e_ref, h_ref, d_ref, k_ref, one_ref, two_ref, out_one_ref, out_two_ref, h1_ref, e1_ref, e0_ref):
    levels, rows, width = one_ref.shape[0], one_ref.shape[1], e_ref.shape[3]
    wide = (rows, width + LANES)
    messages = y_messages(one_ref, two_ref)
    keep = kept_lanes(wide, width)
    zero_row = jnp.zeros((1, wide[1]), jnp.float32)
    zero = jnp.zeros(wide, jnp.float32)
    for z in range(levels):
        for i in range(3):
            e0_ref[i, z] = read_wide(e_ref, i, z, messages, i)
    for z in range(levels):
        above = [e0_ref[i, z + 1] for i in range(2)] if z + 1 < levels else [zero, zero]
        h_here = [read_wide(h_ref, i, z, messages, 3 + i) for i in range(3)]
        new = magnetic([e0_ref[i, z] for i in range(3)], above, h_here, zero_row, zero_row, keep)
        for i in range(3):
            h1_ref[i, z] = new[i]
    inv = []
    for z in range(levels):
        below = [h1_ref[i, z - 1] for i in range(2)] if z else [zero, zero]
        curl = curl_back([h1_ref[i, z] for i in range(3)], below, zero_row, zero_row)
        inv.append(read_wide(k_ref, 0, z, messages, 9))
        for i in range(3):
            e1_ref[i, z] = read_wide(d_ref, i, z, messages, 6 + i) + inv[z] * curl[i]
    even = lax.rem(lax.axis_index("gx"), 2) == 0
    keep_row = kept_lanes((1, wide[1]), width)
    end = slice(rows - 1, rows)
    for z in range(levels):
        hy, hz = h1_ref[1, z, end], h1_ref[2, z, end]
        ex, ey, ez = (e1_ref[i, z, end] for i in range(3))
        up_x = e1_ref[0, z + 1, end] if z + 1 < levels else zero_row
        second_y = hy - COURANT * ((up_x - ex) + ez)
        second_z = hz - COURANT * (-ey - (ahead_y(ex) - ex))
        up = [hy, hz, jnp.where(keep_row, second_y, 0.0), jnp.where(keep_row, second_z, 0.0), inv[z][end]]
        down = [e0_ref[1, z, 0:1], e0_ref[2, z, 0:1], e1_ref[1, z, 0:1], e1_ref[2, z, 0:1], inv[z][0:1]]
        for k in range(5):
            out_one_ref[k, z : z + 1] = jnp.where(even, up[k], down[k])
            out_two_ref[k, z : z + 1] = jnp.where(even, down[k], up[k])


def first_step(e_field, h_field, local, factors, one, two):
    _, levels, rows, width = e_field.shape
    message = jax.ShapeDtypeStruct((5, levels, width + LANES), jnp.float32)
    store = pltpu.VMEM((3, levels, rows, width + LANES), jnp.float32)
    return pl.pallas_call(
        first_body,
        out_shape=(message, message),
        scratch_shapes=[store, store, store],
        compiler_params=VMEM,
        name="first_step",
    )(e_field, h_field, local, factors, one, two)


def both_body(e_ref, h_ref, d_ref, g_ref, k_ref, surface_ref, one_ref, two_ref, x_one_ref, x_two_ref,
              e_out, h_out, ev_ref, ev_low_ref, od_ref, od_low_ref, e0_ref, h1_ref, e1_ref, h2_ref, plane_ref):
    levels, rows, width = one_ref.shape[0], one_ref.shape[1], e_ref.shape[3]
    wide = (rows, width + LANES)
    messages = y_messages(one_ref, two_ref)
    keep = kept_lanes(wide, width)
    keep_row = kept_lanes((1, wide[1]), width)
    zero_row = jnp.zeros((1, wide[1]), jnp.float32)
    zero = jnp.zeros(wide, jnp.float32)
    place, count = lax.axis_index("gx"), lax.axis_size("gx")
    even = lax.rem(place, 2) == 0
    has_before, has_after = place > 0, place < count - 1

    def from_before(k, z):
        got = jnp.where(even, x_two_ref[k, z : z + 1], x_one_ref[k, z : z + 1])
        return jnp.where(has_before, got, 0.0)

    def from_after(k, z):
        got = jnp.where(even, x_one_ref[k, z : z + 1], x_two_ref[k, z : z + 1])
        return jnp.where(has_after, got, 0.0)

    def store_plane(number, layer, part, value):
        at = ((number * 2 + layer) * 4 + part) * rows
        weighted = value[:, :width] * surface_ref[layer].astype(jnp.float32)
        plane_ref[0, at : at + rows] = weighted[:, : width // 2]
        plane_ref[1, at : at + rows] = weighted[:, width // 2 :]

    def layer_of(z):
        return {0: 0, levels - 1: 1}.get(z)

    for z in range(levels):
        for i in range(3):
            e0_ref[i, z] = read_wide(e_ref, i, z, messages, i)
    for z in range(levels):
        above = [e0_ref[i, z + 1] for i in range(2)] if z + 1 < levels else [zero, zero]
        h_here = [read_wide(h_ref, i, z, messages, 3 + i) for i in range(3)]
        new = magnetic(
            [e0_ref[i, z] for i in range(3)], above, h_here, from_after(0, z), from_after(1, z), keep
        )
        for i in range(3):
            h1_ref[i, z] = new[i]
        if layer_of(z) is not None:
            for i in range(2):
                store_plane(0, layer_of(z), 2 + i, new[i])

    first = slice(0, 1)
    end = slice(rows - 1, rows)
    diff_y = [jnp.where(has_before, COURANT * e0_ref[2, z, first], 0.0) for z in range(levels)]
    diff_z = [jnp.where(has_before, -COURANT * e0_ref[1, z, first], 0.0) for z in range(levels)]
    for z in range(levels):
        below = [h1_ref[i, z - 1] for i in range(2)] if z else [zero, zero]
        row_y = from_before(0, z) + diff_y[z]
        row_z = from_before(1, z) + diff_z[z]
        curl = curl_back([h1_ref[i, z] for i in range(3)], below, row_y, row_z)
        inv = read_wide(k_ref, 0, z, messages, 9)
        for i in range(3):
            new = read_wide(d_ref, i, z, messages, 6 + i) + inv * curl[i]
            e1_ref[i, z] = new
            if i < 2 and layer_of(z) is not None:
                store_plane(0, layer_of(z), i, new)

    for z in range(levels):
        above = [e1_ref[i, z + 1] for i in range(2)] if z + 1 < levels else [zero, zero]
        inv = from_after(4, z)
        row_y = from_after(2, z) + inv * h1_ref[2, z, end]
        row_z = from_after(3, z) - inv * h1_ref[1, z, end]
        new = magnetic(
            [e1_ref[i, z] for i in range(3)], above, [h1_ref[i, z] for i in range(3)], row_y, row_z, keep
        )
        for i in range(3):
            h2_ref[i, z] = new[i]
            h_out[i, z] = new[i][:, :width]
        if layer_of(z) is not None:
            for i in range(2):
                store_plane(1, layer_of(z), 2 + i, new[i])

    inv_before = [from_before(4, z) for z in range(levels)]
    diff_ex = []
    for z in range(levels):
        low = diff_y[z - 1] if z else zero_row
        diff_ex.append(inv_before[z] * ((diff_z[z] - behind_y(diff_z[z])) - (diff_y[z] - low)))
    for z in range(levels):
        below = [h2_ref[i, z - 1] for i in range(2)] if z else [zero, zero]
        up = diff_ex[z + 1] if z + 1 < levels else zero_row
        diff_ey = -inv_before[z] * diff_z[z]
        diff_ez = inv_before[z] * diff_y[z]
        row_y = from_before(2, z) + diff_y[z] - COURANT * ((up - diff_ex[z]) - (e1_ref[2, z, first] - diff_ez))
        row_z = from_before(3, z) + diff_z[z] - COURANT * (
            (e1_ref[1, z, first] - diff_ey) - (ahead_y(diff_ex[z]) - diff_ex[z])
        )
        open_row = keep_row & has_before
        row_y = jnp.where(open_row, row_y, 0.0)
        row_z = jnp.where(open_row, row_z, 0.0)
        curl = curl_back([h2_ref[i, z] for i in range(3)], below, row_y, row_z)
        for i in range(3):
            new = k_ref[1, z] * e1_ref[i, z, :, :width] + k_ref[0, z] * curl[i][:, :width] - g_ref[i, z]
            e_out[i, z] = new
            if i < 2 and layer_of(z) is not None:
                store_plane(1, layer_of(z), i, new)

    kinds = 16
    half = width // 2
    back = half - 1 - lane_index((kinds, half))
    for v in range(rows // 2):
        high = [plane_ref[side, pl.ds(rows // 2 + v, kinds, stride=rows), :] for side in range(2)]
        low = [plane_ref[side, pl.ds(rows // 2 - 1 - v, kinds, stride=rows), :] for side in range(2)]
        for parity in range(2):
            left, right = (b - a if parity else b + a for a, b in zip(low, high))
            left = jnp.take_along_axis(left, back, axis=1)
            at = slice((2 * v + parity) * kinds, (2 * v + parity + 1) * kinds)
            for value, ref, low_ref in ((right + left, ev_ref, ev_low_ref), (right - left, od_ref, od_low_ref)):
                top = value.astype(jnp.bfloat16)
                ref[at, :half] = top
                ref[at, half:] = top
                low_ref[at] = (value - top.astype(jnp.float32)).astype(jnp.bfloat16)


def both_steps(e_field, h_field, local, late, factors, surface, one, two, x_one, x_two):
    _, levels, rows, width = e_field.shape
    field = jax.ShapeDtypeStruct(e_field.shape, jnp.float32)
    full = jax.ShapeDtypeStruct((16 * rows, width), jnp.bfloat16)
    part = jax.ShapeDtypeStruct((16 * rows, width // 2), jnp.bfloat16)
    store = pltpu.VMEM((3, levels, rows, width + LANES), jnp.float32)
    return pl.pallas_call(
        both_body,
        out_shape=(field, field, full, part, full, part),
        scratch_shapes=[store, store, store, store, pltpu.VMEM((2, 16 * rows, width // 2), jnp.float32)],
        compiler_params=VMEM,
        name="both_steps",
    )(e_field, h_field, local, late, factors, surface, one, two, x_one, x_two)


def table_body(waves_ref, cos_ref, sin_ref, phase_ref, *, rows, width, scale):
    count = waves_ref.shape[1]
    half = width // 2
    wave_x, wave_y = WAVE * waves_ref[0:1, :], WAVE * waves_ref[1:2, :]
    step = (row_index((8, count)).astype(jnp.float32)) + 0.5
    sin_x, cos_x = sincos(wave_x * step)
    phase_ref[0:8] = cos_x
    phase_ref[8:16] = sin_x
    centre_x = (lax.axis_index("gx") * rows).astype(jnp.float32) + 0.5 * (rows - 1)
    centre_y = (lax.axis_index("gy") * width).astype(jnp.float32) + 0.5 * (width - 1)
    sin_c, cos_c = sincos(wave_x * centre_x + wave_y * centre_y)
    phase_ref[16:24] = jnp.broadcast_to(scale * cos_c, (8, count))
    phase_ref[24:32] = jnp.broadcast_to(scale * sin_c, (8, count))
    sin_y, cos_y = sincos(wave_y * step)
    sin_w, cos_w = sincos(wave_y * 8.0)
    cos_y = jnp.concatenate([cos_y, cos_y * cos_w - sin_y * sin_w], axis=0)
    sin_y = jnp.concatenate([sin_y, sin_y * cos_w + cos_y[0:8] * sin_w], axis=0)
    sin_w, cos_w = 2.0 * sin_w * cos_w, 1.0 - 2.0 * sin_w * sin_w
    for start in range(0, half, 16):
        if start:
            cos_y, sin_y = cos_y * cos_w - sin_y * sin_w, sin_y * cos_w + cos_y * sin_w
        for value, ref in ((cos_y, cos_ref), (sin_y, sin_ref)):
            top = value.astype(jnp.bfloat16)
            ref[start : start + 16] = top
            ref[half + start : half + start + 16] = (value - top.astype(jnp.float32)).astype(jnp.bfloat16)


def tables(waves, rows, width, scale):
    count = waves.shape[1]
    chunk = 256
    table = jax.ShapeDtypeStruct((width, count), jnp.bfloat16)
    block = pl.BlockSpec((width, chunk), lambda i: (0, i))
    return pl.pallas_call(
        partial(table_body, rows=rows, width=width, scale=scale),
        grid=(count // chunk,),
        out_shape=(table, table, jax.ShapeDtypeStruct((32, count), jnp.float32)),
        in_specs=[pl.BlockSpec((2, chunk), lambda i: (0, i))],
        out_specs=(block, block, pl.BlockSpec((32, chunk), lambda i: (0, i))),
        compiler_params=VMEM,
        cost_estimate=pl.CostEstimate(flops=40 * width * count, bytes_accessed=4 * width * count, transcendentals=0),
        name="tables",
    )(waves)


def project_body(ev_ref, ev_low_ref, od_ref, od_low_ref, cos_ref, sin_ref, phase_ref, out_ref):
    half = ev_low_ref.shape[1]
    dot = partial(jnp.dot, preferred_element_type=jnp.float32)
    part_c = dot(ev_ref[...], cos_ref[...]) + dot(ev_low_ref[...], cos_ref[:half])
    part_s = dot(od_ref[...], sin_ref[...]) + dot(od_low_ref[...], sin_ref[:half])
    real = [0.0, 0.0]
    imag = [0.0, 0.0]
    for v in range(8):
        cos_x = phase_ref[v : v + 1]
        sin_x = phase_ref[8 + v : 9 + v]
        for n in range(2):
            same = slice((v * 4 + n) * 8, (v * 4 + n) * 8 + 8)
            flip = slice((v * 4 + 2 + n) * 8, (v * 4 + 2 + n) * 8 + 8)
            real[n] = real[n] + (cos_x * part_c[same] - sin_x * part_s[flip])
            imag[n] = imag[n] + (cos_x * part_s[same] + sin_x * part_c[flip])
    sum_real = 0.0
    sum_imag = 0.0
    for n in range(2):
        cos_n, sin_n = math.cos(OMEGA * (n + 1)), math.sin(OMEGA * (n + 1))
        sum_real = sum_real + (cos_n * real[n] + sin_n * imag[n])
        sum_imag = sum_imag + (cos_n * imag[n] - sin_n * real[n])
    cos_c, sin_c = phase_ref[16:24], phase_ref[24:32]
    out_ref[0:8] = sum_real * cos_c - sum_imag * sin_c
    out_ref[8:16] = sum_real * sin_c + sum_imag * cos_c


def project(planes, cos_y, sin_y, phases, start, count):
    chunk = 512
    ev, ev_low, od, od_low = planes
    width = cos_y.shape[0]
    offset = start // chunk
    whole = lambda a: pl.BlockSpec(a.shape, lambda i: (0, 0))
    table = pl.BlockSpec((width, chunk), lambda i: (0, i + offset))
    return pl.pallas_call(
        project_body,
        grid=(count // chunk,),
        out_shape=jax.ShapeDtypeStruct((16, count), jnp.float32),
        in_specs=[whole(ev), whole(ev_low), whole(od), whole(od_low), table, table,
                  pl.BlockSpec((32, chunk), lambda i: (0, i + offset))],
        out_specs=pl.BlockSpec((16, chunk), lambda i: (0, i)),
        compiler_params=VMEM,
        cost_estimate=pl.CostEstimate(
            flops=8 * ev.shape[0] * width * count, bytes_accessed=4 * width * count, transcendentals=0
        ),
        name="project",
    )(ev, ev_low, od, od_low, cos_y, sin_y, phases)


def swap(array, axis, mask):
    return lax.ppermute(array, axis, [(i, i ^ mask) for i in range(lax.axis_size(axis))])


def swap_other(array, axis):
    count = lax.axis_size(axis)
    return lax.ppermute(array, axis, [(i, (((i + 1) ^ 1) - 1) % count) for i in range(count)])


def bits_of(axis):
    return lax.axis_size(axis).bit_length() - 1


def own_first(directions):
    bits_x, bits_y = bits_of("gx"), bits_of("gy")
    owned = directions.shape[0] // (1 << (bits_x + bits_y))
    waves = directions.T.reshape((2,) + (2,) * (bits_x + bits_y) + (owned,))
    for bit in range(bits_x):
        turn = (lax.axis_index("gx") >> (bits_x - 1 - bit)) & 1
        waves = jnp.where(turn == 1, jnp.flip(waves, 1 + bit), waves)
    for bit in range(bits_y):
        turn = (lax.axis_index("gy") >> (bits_y - 1 - bit)) & 1
        waves = jnp.where(turn == 1, jnp.flip(waves, 1 + bits_x + bit), waves)
    order = [0] + [1 + bits_x + bit for bit in reversed(range(bits_y))]
    order = order + [1 + bit for bit in range(bits_x)] + [1 + bits_x + bits_y]
    return waves.transpose(order).reshape(2, directions.shape[0])


def local(e_field, h_field, pol_now, pol_old, eps_inf, materials, surface, poles, directions):
    _, _, rows, width = e_field.shape
    scale = 1.0 / math.sqrt(rows * lax.axis_size("gx") * width * lax.axis_size("gy"))
    one, two, near, late, factors = prepare(e_field, h_field, pol_now, pol_old, eps_inf, materials, poles)
    one = swap(one, "gy", 1)
    two = swap_other(two, "gy")
    cos_y, sin_y, phases = tables(own_first(directions), rows, width, scale)
    x_one, x_two = first_step(e_field, h_field, near, factors, one, two)
    x_one = swap(x_one, "gx", 1)
    x_two = swap_other(x_two, "gx")
    e_new, h_new, *planes = both_steps(
        e_field, h_field, near, late, factors, surface, one, two, x_one, x_two
    )
    half = directions.shape[0] // 2
    far = project(planes, cos_y, sin_y, phases, half, half)
    arrived = swap(far, "gy", 1)
    far = project(planes, cos_y, sin_y, phases, 0, half) + arrived
    for axis, masks in (("gy", [1 << b for b in range(1, bits_of("gy"))]),
                        ("gx", [1 << b for b in reversed(range(bits_of("gx")))])):
        for mask in masks:
            half = half // 2
            far = far[:, :half] + swap(far[:, half:], axis, mask)
    return e_new, h_new, far.T


def solution(mesh):
    field = P("design", None, "gx", "gy")
    cell = P("design", "gx", "gy")
    return jax.shard_map(
        local,
        mesh=mesh,
        in_specs=(field, field, field, field, cell, cell, cell, P(), P()),
        out_specs=(field, field, P(("gx", "gy"), "design")),
        check_vma=False,
    )
```

```python
from functools import partial
import math

import jax
import jax.numpy as jnp
from jax import lax
from jax.experimental import pallas as pl
from jax.experimental.pallas import tpu as pltpu
from jax.sharding import PartitionSpec as P

COURANT = 0.5
WAVE = 0.3
OMEGA = 0.25
LANES = 128
GROUPS = 4
VMEM = pltpu.CompilerParams(vmem_limit_bytes=24 * 1024 * 1024)


def lane_index(shape):
    return lax.broadcasted_iota(jnp.int32, shape, len(shape) - 1)


def row_index(shape):
    return lax.broadcasted_iota(jnp.int32, shape, 0)


def sincos(angle):
    turns = jnp.round(angle * (0.5 / math.pi))
    rest = angle - turns * 6.28125
    rest = rest - turns * 0.0019350051879882812
    rest = rest - turns * 3.0199159819567e-07
    half = 0.5 * rest
    sq = half * half
    sin_half = 1.0 / 6227020800.0
    for term in (-1.0 / 39916800.0, 1.0 / 362880.0, -1.0 / 5040.0, 1.0 / 120.0, -1.0 / 6.0, 1.0):
        sin_half = sin_half * sq + term
    sin_half = sin_half * half
    cos_half = -1.0 / 87178291200.0
    for term in (1.0 / 479001600.0, -1.0 / 3628800.0, 1.0 / 40320.0, -1.0 / 720.0, 1.0 / 24.0, -0.5, 1.0):
        cos_half = cos_half * sq + term
    return 2.0 * sin_half * cos_half, 1.0 - 2.0 * sin_half * sin_half


def prepare_body(e_in, h_in, p_in, q_in, eps_in, mat_in, poles_in, one_ref, two_ref, d_ref, g_ref, k_ref, e_ref, h_ref,
                 p_ref, q_ref, eps_ref, mat_ref, poles_ref, table_ref, sems, poles_sem):
    levels, rows, width = eps_ref.shape
    last = width - LANES
    pairs = ((e_in, e_ref), (h_in, h_ref), (p_in, p_ref), (q_in, q_ref), (eps_in, eps_ref), (mat_in, mat_ref))
    group = levels // GROUPS
    poles_copy = pltpu.make_async_copy(poles_in, poles_ref, poles_sem)
    poles_copy.start()
    copies = []
    for part in range(GROUPS):
        cut = pl.ds(part * group, group)
        for k, (source, target) in enumerate(pairs):
            at = (slice(None), cut) if len(source.shape) == 4 else (cut,)
            copy = pltpu.make_async_copy(source.at[at], target.at[at], sems.at[part, k])
            copy.start()
            copies.append(copy)
    poles_copy.wait()
    table_ref[0:3, 0 : poles_ref.shape[1]] = poles_ref[...]
    omega_dt, gamma_dt, strength = (table_ref[i : i + 1, :] for i in range(3))
    denominator = 1.0 + 0.5 * gamma_dt
    tile = (rows, LANES)
    table_a = jnp.broadcast_to((2.0 - omega_dt * omega_dt) / denominator, tile)
    table_b = jnp.broadcast_to(-(1.0 - 0.5 * gamma_dt) / denominator, tile)
    table_c = jnp.broadcast_to(strength * omega_dt * omega_dt / denominator, tile)
    lane = lane_index(tile)
    even = lax.rem(lax.axis_index("gy"), 2) == 0
    for z in range(levels):
        if z % group == 0:
            for copy in copies[z // group * 6 : z // group * 6 + 6]:
                copy.wait()
        up = jnp.zeros(tile, jnp.float32)
        down = jnp.zeros(tile, jnp.float32)
        for start in range(0, width, LANES):
            cut = slice(start, start + LANES)
            number = mat_ref[z, :, cut]
            a = jnp.take_along_axis(table_a, number, axis=1)
            b = jnp.take_along_axis(table_b, number, axis=1)
            c = jnp.take_along_axis(table_c, number, axis=1)
            inv = 1.0 / eps_ref[z, :, cut]
            half = COURANT * inv
            k_ref[0, z, :, cut] = half
            k_ref[1, z, :, cut] = 1.0 - c * inv
            items = [e_ref[i, z, :, cut] for i in range(3)] + [h_ref[i, z, :, cut] for i in range(3)]
            for i in range(3):
                now, old = p_ref[i, z, :, cut], q_ref[i, z, :, cut]
                new = a * now + b * old + c * items[i]
                local = items[i] - (new - now) * inv
                d_ref[i, z, :, cut] = local
                g_ref[i, z, :, cut] = ((a * new - new) + b * now) * inv
                items.append(local)
            items.append(half)
            for k, item in enumerate(items):
                if start == 0:
                    moved = pltpu.roll(item, 2 * k, 1) if k else item
                    down = jnp.where((lane >= 2 * k) & (lane < 2 * k + 2), moved, down)
                if start == last:
                    moved = pltpu.roll(item, LANES - 2 * k, 1) if k else item
                    up = jnp.where((lane >= LANES - 2 - 2 * k) & (lane < LANES - 2 * k), moved, up)
        one_ref[z] = jnp.where(even, up, down)
        two_ref[z] = jnp.where(even, down, up)


def prepare(e_field, h_field, pol_now, pol_old, eps_inf, materials, poles):
    levels, rows, width = eps_inf.shape
    message = jax.ShapeDtypeStruct((levels, rows, LANES), jnp.float32)
    field = jax.ShapeDtypeStruct(e_field.shape, jnp.float32)
    pair = jax.ShapeDtypeStruct((2, levels, rows, width), jnp.float32)
    arrays = (e_field, h_field, pol_now, pol_old, eps_inf, materials, poles)
    return pl.pallas_call(
        prepare_body,
        out_shape=(message, message, field, field, pair, field, field),
        in_specs=[pl.BlockSpec(memory_space=pltpu.HBM)] * 7,
        scratch_shapes=[
            pltpu.VMEM(e_field.shape, jnp.float32),
            pltpu.VMEM(e_field.shape, jnp.float32),
            pltpu.VMEM(eps_inf.shape, jnp.float32),
            pltpu.VMEM(eps_inf.shape, jnp.int32),
            pltpu.VMEM(poles.shape, jnp.float32),
            pltpu.VMEM((8, LANES), jnp.float32),
            pltpu.SemaphoreType.DMA((GROUPS, 6)),
            pltpu.SemaphoreType.DMA,
        ],
        compiler_params=VMEM,
        name="prepare",
    )(*(pltpu.with_memory_space_constraint(array, pltpu.HBM) for array in arrays))


def read_wide(own_ref, index, z, messages, item):
    before, after = messages
    lane = lane_index(before[z].shape)
    shift = 2 * item
    late = pltpu.roll(after[z], LANES - shift, 1) if item else after[z]
    early = pltpu.roll(before[z], shift, 1) if item else before[z]
    halo = jnp.where(lane < 2, late, jnp.where(lane >= LANES - 2, early, 0.0))
    return jnp.concatenate([own_ref[index, z], halo], axis=1)


def y_messages(one_ref, two_ref):
    place = lax.axis_index("gy")
    count = lax.axis_size("gy")
    even = lax.rem(place, 2) == 0
    before, after = [], []
    for z in range(one_ref.shape[0]):
        one, two = one_ref[z], two_ref[z]
        before.append(jnp.where(place > 0, jnp.where(even, two, one), 0.0))
        after.append(jnp.where(place < count - 1, jnp.where(even, one, two), 0.0))
    return before, after


def ahead_y(v):
    return pltpu.roll(v, v.shape[1] - 1, 1)


def behind_y(v):
    return pltpu.roll(v, 1, 1)


def ahead_x(v, row):
    at = row_index(v.shape)
    return jnp.where(at == v.shape[0] - 1, row, pltpu.roll(v, v.shape[0] - 1, 0))


def behind_x(v, row):
    at = row_index(v.shape)
    return jnp.where(at == 0, row, pltpu.roll(v, 1, 0))


def magnetic(e_here, e_above, h_here, row_y, row_z, keep):
    ex, ey, ez = e_here
    hx, hy, hz = h_here
    up_x, up_y = e_above
    hx = hx - COURANT * ((ahead_y(ez) - ez) - (up_y - ey))
    hy = hy - COURANT * ((up_x - ex) - (ahead_x(ez, row_z) - ez))
    hz = hz - COURANT * ((ahead_x(ey, row_y) - ey) - (ahead_y(ex) - ex))
    return [jnp.where(keep, v, 0.0) for v in (hx, hy, hz)]


def curl_back(h_here, h_below, row_y, row_z):
    hx, hy, hz = h_here
    low_x, low_y = h_below
    return (
        (hz - behind_y(hz)) - (hy - low_y),
        (hx - low_x) - (hz - behind_x(hz, row_z)),
        (hy - behind_x(hy, row_y)) - (hx - behind_y(hx)),
    )


def kept_lanes(shape, width):
    return (lane_index(shape) < width + LANES // 2) | (lax.axis_index("gy") > 0)


def first_body(e_ref, h_ref, d_ref, k_ref, one_ref, two_ref, out_one_ref, out_two_ref, h1_ref, e1_ref, e0_ref):
    levels, rows, width = one_ref.shape[0], one_ref.shape[1], e_ref.shape[3]
    wide = (rows, width + LANES)
    messages = y_messages(one_ref, two_ref)
    keep = kept_lanes(wide, width)
    zero_row = jnp.zeros((1, wide[1]), jnp.float32)
    zero = jnp.zeros(wide, jnp.float32)
    for z in range(levels):
        for i in range(3):
            e0_ref[i, z] = read_wide(e_ref, i, z, messages, i)
    for z in range(levels):
        above = [e0_ref[i, z + 1] for i in range(2)] if z + 1 < levels else [zero, zero]
        h_here = [read_wide(h_ref, i, z, messages, 3 + i) for i in range(3)]
        new = magnetic([e0_ref[i, z] for i in range(3)], above, h_here, zero_row, zero_row, keep)
        for i in range(3):
            h1_ref[i, z] = new[i]
    inv = []
    for z in range(levels):
        below = [h1_ref[i, z - 1] for i in range(2)] if z else [zero, zero]
        curl = curl_back([h1_ref[i, z] for i in range(3)], below, zero_row, zero_row)
        inv.append(read_wide(k_ref, 0, z, messages, 9))
        for i in range(3):
            e1_ref[i, z] = read_wide(d_ref, i, z, messages, 6 + i) + inv[z] * curl[i]
    even = lax.rem(lax.axis_index("gx"), 2) == 0
    keep_row = kept_lanes((1, wide[1]), width)
    end = slice(rows - 1, rows)
    for z in range(levels):
        hy, hz = h1_ref[1, z, end], h1_ref[2, z, end]
        ex, ey, ez = (e1_ref[i, z, end] for i in range(3))
        up_x = e1_ref[0, z + 1, end] if z + 1 < levels else zero_row
        second_y = hy - COURANT * ((up_x - ex) + ez)
        second_z = hz - COURANT * (-ey - (ahead_y(ex) - ex))
        up = [hy, hz, jnp.where(keep_row, second_y, 0.0), jnp.where(keep_row, second_z, 0.0), inv[z][end]]
        down = [e0_ref[1, z, 0:1], e0_ref[2, z, 0:1], e1_ref[1, z, 0:1], e1_ref[2, z, 0:1], inv[z][0:1]]
        for k in range(5):
            out_one_ref[k, z : z + 1] = jnp.where(even, up[k], down[k])
            out_two_ref[k, z : z + 1] = jnp.where(even, down[k], up[k])


def first_step(e_field, h_field, local, factors, one, two):
    _, levels, rows, width = e_field.shape
    message = jax.ShapeDtypeStruct((5, levels, width + LANES), jnp.float32)
    store = pltpu.VMEM((3, levels, rows, width + LANES), jnp.float32)
    return pl.pallas_call(
        first_body,
        out_shape=(message, message),
        scratch_shapes=[store, store, store],
        compiler_params=VMEM,
        name="first_step",
    )(e_field, h_field, local, factors, one, two)


def both_body(e_ref, h_ref, d_ref, g_ref, k_ref, surface_ref, one_ref, two_ref, x_one_ref, x_two_ref,
              e_out, h_out, ev_ref, ev_low_ref, od_ref, od_low_ref, e0_ref, h1_ref, e1_ref, h2_ref, plane_ref):
    levels, rows, width = one_ref.shape[0], one_ref.shape[1], e_ref.shape[3]
    wide = (rows, width + LANES)
    messages = y_messages(one_ref, two_ref)
    keep = kept_lanes(wide, width)
    keep_row = kept_lanes((1, wide[1]), width)
    zero_row = jnp.zeros((1, wide[1]), jnp.float32)
    zero = jnp.zeros(wide, jnp.float32)
    place, count = lax.axis_index("gx"), lax.axis_size("gx")
    even = lax.rem(place, 2) == 0
    has_before, has_after = place > 0, place < count - 1

    def from_before(k, z):
        got = jnp.where(even, x_two_ref[k, z : z + 1], x_one_ref[k, z : z + 1])
        return jnp.where(has_before, got, 0.0)

    def from_after(k, z):
        got = jnp.where(even, x_one_ref[k, z : z + 1], x_two_ref[k, z : z + 1])
        return jnp.where(has_after, got, 0.0)

    def store_plane(number, layer, part, value):
        at = ((number * 2 + layer) * 4 + part) * rows
        weighted = value[:, :width] * surface_ref[layer].astype(jnp.float32)
        plane_ref[0, at : at + rows] = weighted[:, : width // 2]
        plane_ref[1, at : at + rows] = weighted[:, width // 2 :]

    def layer_of(z):
        return {0: 0, levels - 1: 1}.get(z)

    for z in range(levels):
        for i in range(3):
            e0_ref[i, z] = read_wide(e_ref, i, z, messages, i)
    for z in range(levels):
        above = [e0_ref[i, z + 1] for i in range(2)] if z + 1 < levels else [zero, zero]
        h_here = [read_wide(h_ref, i, z, messages, 3 + i) for i in range(3)]
        new = magnetic(
            [e0_ref[i, z] for i in range(3)], above, h_here, from_after(0, z), from_after(1, z), keep
        )
        for i in range(3):
            h1_ref[i, z] = new[i]
        if layer_of(z) is not None:
            for i in range(2):
                store_plane(0, layer_of(z), 2 + i, new[i])

    first = slice(0, 1)
    end = slice(rows - 1, rows)
    diff_y = [jnp.where(has_before, COURANT * e0_ref[2, z, first], 0.0) for z in range(levels)]
    diff_z = [jnp.where(has_before, -COURANT * e0_ref[1, z, first], 0.0) for z in range(levels)]
    for z in range(levels):
        below = [h1_ref[i, z - 1] for i in range(2)] if z else [zero, zero]
        row_y = from_before(0, z) + diff_y[z]
        row_z = from_before(1, z) + diff_z[z]
        curl = curl_back([h1_ref[i, z] for i in range(3)], below, row_y, row_z)
        inv = read_wide(k_ref, 0, z, messages, 9)
        for i in range(3):
            new = read_wide(d_ref, i, z, messages, 6 + i) + inv * curl[i]
            e1_ref[i, z] = new
            if i < 2 and layer_of(z) is not None:
                store_plane(0, layer_of(z), i, new)

    for z in range(levels):
        above = [e1_ref[i, z + 1] for i in range(2)] if z + 1 < levels else [zero, zero]
        inv = from_after(4, z)
        row_y = from_after(2, z) + inv * h1_ref[2, z, end]
        row_z = from_after(3, z) - inv * h1_ref[1, z, end]
        new = magnetic(
            [e1_ref[i, z] for i in range(3)], above, [h1_ref[i, z] for i in range(3)], row_y, row_z, keep
        )
        for i in range(3):
            h2_ref[i, z] = new[i]
            h_out[i, z] = new[i][:, :width]
        if layer_of(z) is not None:
            for i in range(2):
                store_plane(1, layer_of(z), 2 + i, new[i])

    inv_before = [from_before(4, z) for z in range(levels)]
    diff_ex = []
    for z in range(levels):
        low = diff_y[z - 1] if z else zero_row
        diff_ex.append(inv_before[z] * ((diff_z[z] - behind_y(diff_z[z])) - (diff_y[z] - low)))
    for z in range(levels):
        below = [h2_ref[i, z - 1] for i in range(2)] if z else [zero, zero]
        up = diff_ex[z + 1] if z + 1 < levels else zero_row
        diff_ey = -inv_before[z] * diff_z[z]
        diff_ez = inv_before[z] * diff_y[z]
        row_y = from_before(2, z) + diff_y[z] - COURANT * ((up - diff_ex[z]) - (e1_ref[2, z, first] - diff_ez))
        row_z = from_before(3, z) + diff_z[z] - COURANT * (
            (e1_ref[1, z, first] - diff_ey) - (ahead_y(diff_ex[z]) - diff_ex[z])
        )
        open_row = keep_row & has_before
        row_y = jnp.where(open_row, row_y, 0.0)
        row_z = jnp.where(open_row, row_z, 0.0)
        curl = curl_back([h2_ref[i, z] for i in range(3)], below, row_y, row_z)
        for i in range(3):
            new = k_ref[1, z] * e1_ref[i, z, :, :width] + k_ref[0, z] * curl[i][:, :width] - g_ref[i, z]
            e_out[i, z] = new
            if i < 2 and layer_of(z) is not None:
                store_plane(1, layer_of(z), i, new)

    kinds = 16
    half = width // 2
    back = half - 1 - lane_index((kinds, half))
    for v in range(rows // 2):
        high = [plane_ref[side, pl.ds(rows // 2 + v, kinds, stride=rows), :] for side in range(2)]
        low = [plane_ref[side, pl.ds(rows // 2 - 1 - v, kinds, stride=rows), :] for side in range(2)]
        for parity in range(2):
            left, right = (b - a if parity else b + a for a, b in zip(low, high))
            left = jnp.take_along_axis(left, back, axis=1)
            at = slice((2 * v + parity) * kinds, (2 * v + parity + 1) * kinds)
            for value, ref, low_ref in ((right + left, ev_ref, ev_low_ref), (right - left, od_ref, od_low_ref)):
                top = value.astype(jnp.bfloat16)
                ref[at, :half] = top
                ref[at, half:] = top
                low_ref[at] = (value - top.astype(jnp.float32)).astype(jnp.bfloat16)


def both_steps(e_field, h_field, local, late, factors, surface, one, two, x_one, x_two):
    _, levels, rows, width = e_field.shape
    field = jax.ShapeDtypeStruct(e_field.shape, jnp.float32)
    full = jax.ShapeDtypeStruct((16 * rows, width), jnp.bfloat16)
    part = jax.ShapeDtypeStruct((16 * rows, width // 2), jnp.bfloat16)
    store = pltpu.VMEM((3, levels, rows, width + LANES), jnp.float32)
    return pl.pallas_call(
        both_body,
        out_shape=(field, field, full, part, full, part),
        scratch_shapes=[store, store, store, store, pltpu.VMEM((2, 16 * rows, width // 2), jnp.float32)],
        compiler_params=VMEM,
        name="both_steps",
    )(e_field, h_field, local, late, factors, surface, one, two, x_one, x_two)


def table_body(waves_ref, cos_ref, sin_ref, phase_ref, *, rows, width, scale):
    half = width // 2
    chunk = 256
    step = (row_index((8, chunk)).astype(jnp.float32)) + 0.5
    centre_x = (lax.axis_index("gx") * rows).astype(jnp.float32) + 0.5 * (rows - 1)
    centre_y = (lax.axis_index("gy") * width).astype(jnp.float32) + 0.5 * (width - 1)

    @pl.loop(0, waves_ref.shape[1] // chunk)
    def _(turn):
        cut = pl.ds(pl.multiple_of(turn * chunk, chunk), chunk)
        wave_x, wave_y = WAVE * waves_ref[0:1, cut], WAVE * waves_ref[1:2, cut]
        sin_x, cos_x = sincos(wave_x * step)
        phase_ref[0:8, cut] = cos_x
        phase_ref[8:16, cut] = sin_x
        sin_c, cos_c = sincos(wave_x * centre_x + wave_y * centre_y)
        phase_ref[16:24, cut] = jnp.broadcast_to(scale * cos_c, step.shape)
        phase_ref[24:32, cut] = jnp.broadcast_to(scale * sin_c, step.shape)
        sin_y, cos_y = sincos(wave_y * step)
        sin_w, cos_w = sincos(wave_y * 8.0)
        cos_y = jnp.concatenate([cos_y, cos_y * cos_w - sin_y * sin_w], axis=0)
        sin_y = jnp.concatenate([sin_y, sin_y * cos_w + cos_y[0:8] * sin_w], axis=0)
        sin_w, cos_w = 2.0 * sin_w * cos_w, 1.0 - 2.0 * sin_w * sin_w
        for start in range(0, half, 16):
            if start:
                cos_y, sin_y = cos_y * cos_w - sin_y * sin_w, sin_y * cos_w + cos_y * sin_w
            for value, ref in ((cos_y, cos_ref), (sin_y, sin_ref)):
                top = value.astype(jnp.bfloat16)
                ref[start : start + 16, cut] = top
                ref[half + start : half + start + 16, cut] = (value - top.astype(jnp.float32)).astype(jnp.bfloat16)


def tables(waves, rows, width, scale):
    count = waves.shape[1]
    table = jax.ShapeDtypeStruct((width, count), jnp.bfloat16)
    return pl.pallas_call(
        partial(table_body, rows=rows, width=width, scale=scale),
        out_shape=(table, table, jax.ShapeDtypeStruct((32, count), jnp.float32)),
        compiler_params=VMEM,
        cost_estimate=pl.CostEstimate(flops=40 * width * count, bytes_accessed=4 * width * count, transcendentals=0),
        name="tables",
    )(waves)


def project_body(ev_ref, ev_low_ref, od_ref, od_low_ref, cos_ref, sin_ref, phase_ref, out_ref, *, start):
    half = ev_low_ref.shape[1]
    chunk = 256
    dot = partial(jnp.dot, preferred_element_type=jnp.float32)
    for at in range(0, out_ref.shape[1], chunk):
        cut = slice(start + at, start + at + chunk)
        part_c = dot(ev_ref[...], cos_ref[:, cut]) + dot(ev_low_ref[...], cos_ref[:half, cut])
        part_s = dot(od_ref[...], sin_ref[:, cut]) + dot(od_low_ref[...], sin_ref[:half, cut])
        real = [0.0, 0.0]
        imag = [0.0, 0.0]
        for v in range(8):
            cos_x = phase_ref[v : v + 1, cut]
            sin_x = phase_ref[8 + v : 9 + v, cut]
            for n in range(2):
                same = slice((v * 4 + n) * 8, (v * 4 + n) * 8 + 8)
                flip = slice((v * 4 + 2 + n) * 8, (v * 4 + 2 + n) * 8 + 8)
                real[n] = real[n] + (cos_x * part_c[same] - sin_x * part_s[flip])
                imag[n] = imag[n] + (cos_x * part_s[same] + sin_x * part_c[flip])
        sum_real = 0.0
        sum_imag = 0.0
        for n in range(2):
            cos_n, sin_n = math.cos(OMEGA * (n + 1)), math.sin(OMEGA * (n + 1))
            sum_real = sum_real + (cos_n * real[n] + sin_n * imag[n])
            sum_imag = sum_imag + (cos_n * imag[n] - sin_n * real[n])
        cos_c, sin_c = phase_ref[16:24, cut], phase_ref[24:32, cut]
        out_ref[0:8, at : at + chunk] = sum_real * cos_c - sum_imag * sin_c
        out_ref[8:16, at : at + chunk] = sum_real * sin_c + sum_imag * cos_c


def project(planes, cos_y, sin_y, phases, start, count):
    ev, ev_low, od, od_low = planes
    width = cos_y.shape[0]
    return pl.pallas_call(
        partial(project_body, start=start),
        out_shape=jax.ShapeDtypeStruct((16, count), jnp.float32),
        compiler_params=VMEM,
        cost_estimate=pl.CostEstimate(
            flops=8 * ev.shape[0] * width * count, bytes_accessed=4 * width * count, transcendentals=0
        ),
        name="project",
    )(ev, ev_low, od, od_low, cos_y, sin_y, phases)


def swap(array, axis, mask):
    return lax.ppermute(array, axis, [(i, i ^ mask) for i in range(lax.axis_size(axis))])


def swap_other(array, axis):
    pairs = [(i, ((i + 1) ^ 1) - 1) for i in range(1, lax.axis_size(axis) - 1)]
    return lax.ppermute(array, axis, pairs)


def bits_of(axis):
    return lax.axis_size(axis).bit_length() - 1


def own_first(directions):
    bits_x, bits_y = bits_of("gx"), bits_of("gy")
    owned = directions.shape[0] // (1 << (bits_x + bits_y))
    waves = directions.T.reshape((2,) + (2,) * (bits_x + bits_y) + (owned,))
    for bit in range(bits_x):
        turn = (lax.axis_index("gx") >> (bits_x - 1 - bit)) & 1
        waves = jnp.where(turn == 1, jnp.flip(waves, 1 + bit), waves)
    for bit in range(bits_y):
        turn = (lax.axis_index("gy") >> (bits_y - 1 - bit)) & 1
        waves = jnp.where(turn == 1, jnp.flip(waves, 1 + bits_x + bit), waves)
    order = [0] + [1 + bits_x + bit for bit in reversed(range(bits_y))]
    order = order + [1 + bit for bit in range(bits_x)] + [1 + bits_x + bits_y]
    return waves.transpose(order).reshape(2, directions.shape[0])


def local(e_field, h_field, pol_now, pol_old, eps_inf, materials, surface, poles, directions):
    _, _, rows, width = e_field.shape
    scale = 1.0 / math.sqrt(rows * lax.axis_size("gx") * width * lax.axis_size("gy"))
    one, two, near, late, factors, e_field, h_field = prepare(e_field, h_field, pol_now, pol_old, eps_inf, materials, poles)
    one = swap(one, "gy", 1)
    two = swap_other(two, "gy")
    cos_y, sin_y, phases = tables(own_first(directions), rows, width, scale)
    x_one, x_two = first_step(e_field, h_field, near, factors, one, two)
    x_one = swap(x_one, "gx", 1)
    x_two = swap_other(x_two, "gx")
    e_new, h_new, *planes = both_steps(
        e_field, h_field, near, late, factors, surface, one, two, x_one, x_two
    )
    half = directions.shape[0] // 2
    far = project(planes, cos_y, sin_y, phases, half, half)
    arrived = swap(far, "gy", 1)
    far = project(planes, cos_y, sin_y, phases, 0, half) + arrived
    for axis, masks in (("gy", [1 << b for b in range(1, bits_of("gy"))]),
                        ("gx", [1 << b for b in reversed(range(bits_of("gx")))])):
        for mask in masks:
            half = half // 2
            far = far[:, :half] + swap(far[:, half:], axis, mask)
    return e_new, h_new, far.T


def solution(mesh):
    field = P("design", None, "gx", "gy")
    cell = P("design", "gx", "gy")
    return jax.shard_map(
        local,
        mesh=mesh,
        in_specs=(field, field, field, field, cell, cell, cell, P(), P()),
        out_specs=(field, field, P(("gx", "gy"), "design")),
        check_vma=False,
    )
```

```python
from functools import partial
import math

import jax
import jax.numpy as jnp
from jax import lax
from jax.experimental import pallas as pl
from jax.experimental.pallas import tpu as pltpu
from jax.sharding import PartitionSpec as P

COURANT = 0.5
WAVE = 0.3
OMEGA = 0.25
LANES = 128
GROUPS = 4
SLOTS = 24
VMEM = pltpu.CompilerParams(vmem_limit_bytes=24 * 1024 * 1024)


def lane_index(shape):
    return lax.broadcasted_iota(jnp.int32, shape, len(shape) - 1)


def row_index(shape):
    return lax.broadcasted_iota(jnp.int32, shape, 0)


def sincos(angle):
    turns = jnp.round(angle * (0.5 / math.pi))
    rest = angle - turns * 6.28125
    rest = rest - turns * 0.0019350051879882812
    rest = rest - turns * 3.0199159819567e-07
    half = 0.5 * rest
    sq = half * half
    sin_half = 1.0 / 6227020800.0
    for term in (-1.0 / 39916800.0, 1.0 / 362880.0, -1.0 / 5040.0, 1.0 / 120.0, -1.0 / 6.0, 1.0):
        sin_half = sin_half * sq + term
    sin_half = sin_half * half
    cos_half = -1.0 / 87178291200.0
    for term in (1.0 / 479001600.0, -1.0 / 3628800.0, 1.0 / 40320.0, -1.0 / 720.0, 1.0 / 24.0, -0.5, 1.0):
        cos_half = cos_half * sq + term
    return 2.0 * sin_half * cos_half, 1.0 - 2.0 * sin_half * sin_half


def prepare_body(e_in, h_in, p_in, q_in, eps_in, mat_in, poles_in, one_ref, two_ref, d_ref, g_ref, k_ref, e_ref, h_ref,
                 p_ref, q_ref, eps_ref, mat_ref, poles_ref, table_ref, up_ref, down_ref, sems, poles_sem):
    levels, rows, width = eps_ref.shape
    last = width - LANES
    pairs = ((e_in, e_ref), (h_in, h_ref), (p_in, p_ref), (q_in, q_ref), (eps_in, eps_ref), (mat_in, mat_ref))
    group = levels // GROUPS
    poles_copy = pltpu.make_async_copy(poles_in, poles_ref, poles_sem)
    poles_copy.start()
    copies = []
    for part in range(GROUPS):
        cut = pl.ds(part * group, group)
        for k, (source, target) in enumerate(pairs):
            at = (slice(None), cut) if len(source.shape) == 4 else (cut,)
            copy = pltpu.make_async_copy(source.at[at], target.at[at], sems.at[part, k])
            copy.start()
            copies.append(copy)
    poles_copy.wait()
    table_ref[0:3, 0 : poles_ref.shape[1]] = poles_ref[...]
    omega_dt, gamma_dt, strength = (table_ref[i : i + 1, :] for i in range(3))
    denominator = 1.0 + 0.5 * gamma_dt
    tile = (rows, LANES)
    table_a = jnp.broadcast_to((2.0 - omega_dt * omega_dt) / denominator, tile)
    table_b = jnp.broadcast_to(-(1.0 - 0.5 * gamma_dt) / denominator, tile)
    table_c = jnp.broadcast_to(strength * omega_dt * omega_dt / denominator, tile)
    lane = lane_index(tile)
    even = lax.rem(lax.axis_index("gy"), 2) == 0
    for z in range(levels):
        if z % group == 0:
            for copy in copies[z // group * 6 : z // group * 6 + 6]:
                copy.wait()
        up = jnp.zeros(tile, jnp.float32)
        down = jnp.zeros(tile, jnp.float32)
        for start in range(0, width, LANES):
            cut = slice(start, start + LANES)
            number = mat_ref[z, :, cut]
            a = jnp.take_along_axis(table_a, number, axis=1)
            b = jnp.take_along_axis(table_b, number, axis=1)
            c = jnp.take_along_axis(table_c, number, axis=1)
            inv = 1.0 / eps_ref[z, :, cut]
            half = COURANT * inv
            k_ref[0, z, :, cut] = half
            k_ref[1, z, :, cut] = 1.0 - c * inv
            items = [e_ref[i, z, :, cut] for i in range(3)] + [h_ref[i, z, :, cut] for i in range(3)]
            for i in range(3):
                now, old = p_ref[i, z, :, cut], q_ref[i, z, :, cut]
                new = a * now + b * old + c * items[i]
                local = items[i] - (new - now) * inv
                d_ref[i, z, :, cut] = local
                g_ref[i, z, :, cut] = ((a * new - new) + b * now) * inv
                items.append(local)
            items.append(half)
            for k, item in enumerate(items):
                if start == 0:
                    moved = pltpu.roll(item, 2 * k, 1) if k else item
                    down = jnp.where((lane >= 2 * k) & (lane < 2 * k + 2), moved, down)
                if start == last:
                    moved = pltpu.roll(item, LANES - 2 * k, 1) if k else item
                    up = jnp.where((lane >= LANES - 2 - 2 * k) & (lane < LANES - 2 * k), moved, up)
        up_ref[z * rows : (z + 1) * rows] = up
        down_ref[z * rows : (z + 1) * rows] = down
    up = up_ref[...].T[LANES - SLOTS :]
    down = down_ref[...].T[:SLOTS]
    one_ref[...] = jnp.where(even, up, down)
    two_ref[...] = jnp.where(even, down, up)


def prepare(e_field, h_field, pol_now, pol_old, eps_inf, materials, poles):
    levels, rows, width = eps_inf.shape
    message = jax.ShapeDtypeStruct((SLOTS, levels * rows), jnp.float32)
    field = jax.ShapeDtypeStruct(e_field.shape, jnp.float32)
    pair = jax.ShapeDtypeStruct((2, levels, rows, width), jnp.float32)
    arrays = (e_field, h_field, pol_now, pol_old, eps_inf, materials, poles)
    return pl.pallas_call(
        prepare_body,
        out_shape=(message, message, field, field, pair, field, field),
        in_specs=[pl.BlockSpec(memory_space=pltpu.HBM)] * 7,
        scratch_shapes=[
            pltpu.VMEM(e_field.shape, jnp.float32),
            pltpu.VMEM(e_field.shape, jnp.float32),
            pltpu.VMEM(eps_inf.shape, jnp.float32),
            pltpu.VMEM(eps_inf.shape, jnp.int32),
            pltpu.VMEM(poles.shape, jnp.float32),
            pltpu.VMEM((8, LANES), jnp.float32),
            pltpu.VMEM((levels * rows, LANES), jnp.float32),
            pltpu.VMEM((levels * rows, LANES), jnp.float32),
            pltpu.SemaphoreType.DMA((GROUPS, 6)),
            pltpu.SemaphoreType.DMA,
        ],
        compiler_params=VMEM,
        name="prepare",
    )(*(pltpu.with_memory_space_constraint(array, pltpu.HBM) for array in arrays))


def read_wide(own_ref, index, z, halo_ref, item):
    both = halo_ref[z]
    lane = lane_index(both.shape)
    shift = 2 * item
    late = pltpu.roll(both, LANES - shift, 1) if item else both
    early = pltpu.roll(both, shift, 1) if item else both
    halo = jnp.where(lane < 2, late, jnp.where(lane >= LANES - 2, early, 0.0))
    return jnp.concatenate([own_ref[index, z], halo], axis=1)


def read_y_messages(one_ref, two_ref, halo_ref):
    place = lax.axis_index("gy")
    even = lax.rem(place, 2) == 0
    one, two = one_ref[...], two_ref[...]
    before = jnp.where(place > 0, jnp.where(even, two, one), 0.0)
    after = jnp.where(place < lax.axis_size("gy") - 1, jnp.where(even, one, two), 0.0)
    blank = jnp.zeros((LANES - 2 * SLOTS, one.shape[1]), jnp.float32)
    halo_ref[...] = jnp.concatenate([after, blank, before], axis=0).T.reshape(halo_ref.shape)


def ahead_y(v):
    return pltpu.roll(v, v.shape[1] - 1, 1)


def behind_y(v):
    return pltpu.roll(v, 1, 1)


def ahead_x(v, row):
    at = row_index(v.shape)
    return jnp.where(at == v.shape[0] - 1, row, pltpu.roll(v, v.shape[0] - 1, 0))


def behind_x(v, row):
    at = row_index(v.shape)
    return jnp.where(at == 0, row, pltpu.roll(v, 1, 0))


def magnetic(e_here, e_above, h_here, row_y, row_z, keep):
    ex, ey, ez = e_here
    hx, hy, hz = h_here
    up_x, up_y = e_above
    hx = hx - COURANT * ((ahead_y(ez) - ez) - (up_y - ey))
    hy = hy - COURANT * ((up_x - ex) - (ahead_x(ez, row_z) - ez))
    hz = hz - COURANT * ((ahead_x(ey, row_y) - ey) - (ahead_y(ex) - ex))
    return [jnp.where(keep, v, 0.0) for v in (hx, hy, hz)]


def curl_back(h_here, h_below, row_y, row_z):
    hx, hy, hz = h_here
    low_x, low_y = h_below
    return (
        (hz - behind_y(hz)) - (hy - low_y),
        (hx - low_x) - (hz - behind_x(hz, row_z)),
        (hy - behind_x(hy, row_y)) - (hx - behind_y(hx)),
    )


def kept_lanes(shape, width):
    return (lane_index(shape) < width + LANES // 2) | (lax.axis_index("gy") > 0)


def first_body(e_ref, h_ref, d_ref, k_ref, one_ref, two_ref, tie_ref, out_one_ref, out_two_ref, h1_ref, e1_ref, e0_ref, halo_ref):
    del tie_ref
    _, levels, rows, width = e_ref.shape
    wide = (rows, width + LANES)
    read_y_messages(one_ref, two_ref, halo_ref)
    keep = kept_lanes(wide, width)
    zero_row = jnp.zeros((1, wide[1]), jnp.float32)
    zero = jnp.zeros(wide, jnp.float32)
    for z in range(levels):
        for i in range(3):
            e0_ref[i, z] = read_wide(e_ref, i, z, halo_ref, i)
    for z in range(levels):
        above = [e0_ref[i, z + 1] for i in range(2)] if z + 1 < levels else [zero, zero]
        h_here = [read_wide(h_ref, i, z, halo_ref, 3 + i) for i in range(3)]
        new = magnetic([e0_ref[i, z] for i in range(3)], above, h_here, zero_row, zero_row, keep)
        for i in range(3):
            h1_ref[i, z] = new[i]
    inv = []
    for z in range(levels):
        below = [h1_ref[i, z - 1] for i in range(2)] if z else [zero, zero]
        curl = curl_back([h1_ref[i, z] for i in range(3)], below, zero_row, zero_row)
        inv.append(read_wide(k_ref, 0, z, halo_ref, 9))
        for i in range(3):
            e1_ref[i, z] = read_wide(d_ref, i, z, halo_ref, 6 + i) + inv[z] * curl[i]
    even = lax.rem(lax.axis_index("gx"), 2) == 0
    keep_row = kept_lanes((1, wide[1]), width)
    end = slice(rows - 1, rows)
    for z in range(levels):
        hy, hz = h1_ref[1, z, end], h1_ref[2, z, end]
        ex, ey, ez = (e1_ref[i, z, end] for i in range(3))
        up_x = e1_ref[0, z + 1, end] if z + 1 < levels else zero_row
        second_y = hy - COURANT * ((up_x - ex) + ez)
        second_z = hz - COURANT * (-ey - (ahead_y(ex) - ex))
        up = [hy, hz, jnp.where(keep_row, second_y, 0.0), jnp.where(keep_row, second_z, 0.0), inv[z][end]]
        down = [e0_ref[1, z, 0:1], e0_ref[2, z, 0:1], e1_ref[1, z, 0:1], e1_ref[2, z, 0:1], inv[z][0:1]]
        for k in range(5):
            out_one_ref[k, z : z + 1] = jnp.where(even, up[k], down[k])
            out_two_ref[k, z : z + 1] = jnp.where(even, down[k], up[k])


def first_step(e_field, h_field, local, factors, one, two, tie):
    _, levels, rows, width = e_field.shape
    message = jax.ShapeDtypeStruct((5, levels, width + LANES), jnp.float32)
    store = (3, levels, rows, width + LANES)
    field = jax.ShapeDtypeStruct(store, jnp.float32)
    vmem = pl.BlockSpec(memory_space=pltpu.VMEM)
    return pl.pallas_call(
        first_body,
        out_shape=(message, message, field, field),
        in_specs=[vmem] * 6 + [pl.BlockSpec(memory_space=pl.ANY)],
        scratch_shapes=[pltpu.VMEM(store, jnp.float32), pltpu.VMEM((levels, rows, LANES), jnp.float32)],
        compiler_params=VMEM,
        name="first_step",
    )(e_field, h_field, local, factors, one, two, tie)


def store_plane(plane_ref, surface_ref, number, layer, part, value):
    rows, half = value.shape[0], plane_ref.shape[2]
    at = ((number * 2 + layer) * 4 + part) * rows
    weighted = value[:, : 2 * half] * surface_ref[layer].astype(jnp.float32)
    plane_ref[0, at : at + rows] = weighted[:, :half]
    plane_ref[1, at : at + rows] = weighted[:, half:]


def split_planes(plane_ref, split_refs, rows, pairs):
    ev_ref, ev_low_ref, od_ref, od_low_ref = split_refs
    kinds = 16
    half = plane_ref.shape[2]
    back = half - 1 - lane_index((kinds, half))
    for turn, v in enumerate(pairs):
        high = [plane_ref[side, pl.ds(rows // 2 + v, kinds, stride=rows), :] for side in range(2)]
        low = [plane_ref[side, pl.ds(rows // 2 - 1 - v, kinds, stride=rows), :] for side in range(2)]
        for parity in range(2):
            left, right = (b - a if parity else b + a for a, b in zip(low, high))
            left = jnp.take_along_axis(left, back, axis=1)
            at = slice((2 * turn + parity) * kinds, (2 * turn + parity + 1) * kinds)
            for value, ref, low_ref in ((right + left, ev_ref, ev_low_ref), (right - left, od_ref, od_low_ref)):
                top = value.astype(jnp.bfloat16)
                ref[at, :half] = top
                ref[at, half:] = top
                low_ref[at] = (value - top.astype(jnp.float32)).astype(jnp.bfloat16)


def project_chunk(split_refs, cos_ref, sin_ref, phase_ref, cut, pairs):
    ev_ref, ev_low_ref, od_ref, od_low_ref = split_refs
    half = ev_low_ref.shape[1]
    dot = partial(jnp.dot, preferred_element_type=jnp.float32)
    part_c = dot(ev_ref[...], cos_ref[:, cut]) + dot(ev_low_ref[...], cos_ref[:half, cut])
    part_s = dot(od_ref[...], sin_ref[:, cut]) + dot(od_low_ref[...], sin_ref[:half, cut])
    real = [0.0, 0.0]
    imag = [0.0, 0.0]
    for turn, v in enumerate(pairs):
        cos_x = phase_ref[v : v + 1, cut]
        sin_x = phase_ref[8 + v : 9 + v, cut]
        for n in range(2):
            same = slice((turn * 4 + n) * 8, (turn * 4 + n) * 8 + 8)
            flip = slice((turn * 4 + 2 + n) * 8, (turn * 4 + 2 + n) * 8 + 8)
            real[n] = real[n] + (cos_x * part_c[same] - sin_x * part_s[flip])
            imag[n] = imag[n] + (cos_x * part_s[same] + sin_x * part_c[flip])
    sum_real = 0.0
    sum_imag = 0.0
    for n in range(2):
        cos_n, sin_n = math.cos(OMEGA * (n + 1)), math.sin(OMEGA * (n + 1))
        sum_real = sum_real + (cos_n * real[n] + sin_n * imag[n])
        sum_imag = sum_imag + (cos_n * imag[n] - sin_n * real[n])
    cos_c, sin_c = phase_ref[16:24, cut], phase_ref[24:32, cut]
    return sum_real * cos_c - sum_imag * sin_c, sum_real * sin_c + sum_imag * cos_c


def split_shapes(pairs, width):
    count = 32 * len(pairs)
    return [(count, width), (count, width // 2)] * 2


def inside_body(h1_ref, e1_ref, g_ref, k_ref, surface_ref, cos_ref, sin_ref, phase_ref, out_ref, plane_ref, *split_refs, pairs):
    _, levels, rows, _ = h1_ref.shape
    width = g_ref.shape[3]
    wide = (rows, h1_ref.shape[3])
    keep = kept_lanes(wide, width)
    zero_row = jnp.zeros((1, wide[1]), jnp.float32)
    zero = jnp.zeros(wide, jnp.float32)

    def second(z):
        above = [e1_ref[i, z + 1] for i in range(2)] if z + 1 < levels else [zero, zero]
        here = [e1_ref[i, z] for i in range(3)]
        return magnetic(here, above, [h1_ref[i, z] for i in range(3)], zero_row, zero_row, keep)

    for layer, z in enumerate((0, levels - 1)):
        h2 = second(z)
        below = second(z - 1)[:2] if z else [zero, zero]
        curl = curl_back(h2, below, zero_row, zero_row)
        for i in range(2):
            store_plane(plane_ref, surface_ref, 0, layer, i, e1_ref[i, z])
            store_plane(plane_ref, surface_ref, 0, layer, 2 + i, h1_ref[i, z])
            new = k_ref[1, z] * e1_ref[i, z, :, :width] + k_ref[0, z] * curl[i][:, :width] - g_ref[i, z]
            store_plane(plane_ref, surface_ref, 1, layer, i, new)
            store_plane(plane_ref, surface_ref, 1, layer, 2 + i, h2[i])
    split_planes(plane_ref, split_refs, rows, pairs)
    chunk = 256
    for at in range(0, out_ref.shape[1], chunk):
        cut = slice(at, at + chunk)
        out_ref[0:8, cut], out_ref[8:16, cut] = project_chunk(split_refs, cos_ref, sin_ref, phase_ref, cut, pairs)


def inside(h1, e1, late, factors, surface, cos_y, sin_y, phases):
    _, _, rows, width = late.shape
    pairs = range(rows // 2 - 2)
    count = cos_y.shape[1]
    return pl.pallas_call(
        partial(inside_body, pairs=pairs),
        out_shape=jax.ShapeDtypeStruct((16, count), jnp.float32),
        scratch_shapes=[pltpu.VMEM((2, 16 * rows, width // 2), jnp.float32)]
        + [pltpu.VMEM(shape, jnp.bfloat16) for shape in split_shapes(pairs, width)],
        compiler_params=VMEM,
        cost_estimate=pl.CostEstimate(
            flops=8 * 32 * len(pairs) * width * count, bytes_accessed=4 * width * count, transcendentals=0
        ),
        name="inside",
    )(h1, e1, late, factors, surface, cos_y, sin_y, phases)


def second_body(h1_in, e1_in, g_ref, k_ref, surface_ref, own_one_ref, own_two_ref, x_one_ref, x_two_ref, e_out, h_out,
                ev_ref, ev_low_ref, od_ref, od_low_ref, h1_ref, e1_ref, h2_ref, plane_ref, *, pairs):
    _, levels, rows, _ = h1_in.shape
    width = g_ref.shape[3]
    wide = (rows, h1_in.shape[3])
    keep = kept_lanes(wide, width)
    keep_row = kept_lanes((1, wide[1]), width)
    zero_row = jnp.zeros((1, wide[1]), jnp.float32)
    zero = jnp.zeros(wide, jnp.float32)
    at_row = row_index(wide)
    place, count = lax.axis_index("gx"), lax.axis_size("gx")
    even = lax.rem(place, 2) == 0
    has_before, has_after = place > 0, place < count - 1
    first, end = slice(0, 1), slice(rows - 1, rows)
    layers = {0: 0, levels - 1: 1}

    def from_before(k, z):
        got = jnp.where(even, x_two_ref[k, z : z + 1], x_one_ref[k, z : z + 1])
        return jnp.where(has_before, got, 0.0)

    def from_after(k, z):
        got = jnp.where(even, x_one_ref[k, z : z + 1], x_two_ref[k, z : z + 1])
        return jnp.where(has_after, got, 0.0)

    def own_up(k, z):
        return jnp.where(even, own_one_ref[k, z : z + 1], own_two_ref[k, z : z + 1])

    def own_down(k, z):
        return jnp.where(even, own_two_ref[k, z : z + 1], own_one_ref[k, z : z + 1])

    def patched(value, start, stop):
        if start is not None:
            value = jnp.where(at_row == 0, value + start, value)
        return jnp.where(at_row == rows - 1, value + stop, value)

    diff_y = [jnp.where(has_before, COURANT * own_down(1, z), 0.0) for z in range(levels)]
    diff_z = [jnp.where(has_before, -COURANT * own_down(0, z), 0.0) for z in range(levels)]
    last_y = [COURANT * from_after(1, z) for z in range(levels)]
    last_z = [-COURANT * from_after(0, z) for z in range(levels)]
    for z in range(levels):
        h1 = [h1_in[0, z], patched(h1_in[1, z], None, last_y[z]), patched(h1_in[2, z], None, last_z[z])]
        low = last_y[z - 1] if z else zero_row
        inv, inv_first = own_up(4, z), own_down(4, z)
        stop_x = inv * ((last_z[z] - behind_y(last_z[z])) - (last_y[z] - low))
        start_y = inv_first * (from_before(1, z) + diff_z[z])
        start_z = -inv_first * (from_before(0, z) + diff_y[z])
        e1 = [
            patched(e1_in[0, z], None, stop_x),
            patched(e1_in[1, z], start_y, -inv * last_z[z]),
            patched(e1_in[2, z], start_z, inv * last_y[z]),
        ]
        for i in range(3):
            h1_ref[i, z] = h1[i]
            e1_ref[i, z] = e1[i]
        if z in layers:
            for i in range(2):
                store_plane(plane_ref, surface_ref, 0, layers[z], i, e1[i])
                store_plane(plane_ref, surface_ref, 0, layers[z], 2 + i, h1[i])

    for z in range(levels):
        above = [e1_ref[i, z + 1] for i in range(2)] if z + 1 < levels else [zero, zero]
        inv = from_after(4, z)
        row_y = from_after(2, z) + inv * h1_ref[2, z, end]
        row_z = from_after(3, z) - inv * h1_ref[1, z, end]
        new = magnetic(
            [e1_ref[i, z] for i in range(3)], above, [h1_ref[i, z] for i in range(3)], row_y, row_z, keep
        )
        for i in range(3):
            h2_ref[i, z] = new[i]
            h_out[i, z] = new[i][:, :width]
        if z in layers:
            for i in range(2):
                store_plane(plane_ref, surface_ref, 1, layers[z], 2 + i, new[i])

    inv_before = [from_before(4, z) for z in range(levels)]
    diff_ex = []
    for z in range(levels):
        low = diff_y[z - 1] if z else zero_row
        diff_ex.append(inv_before[z] * ((diff_z[z] - behind_y(diff_z[z])) - (diff_y[z] - low)))
    for z in range(levels):
        below = [h2_ref[i, z - 1] for i in range(2)] if z else [zero, zero]
        up = diff_ex[z + 1] if z + 1 < levels else zero_row
        diff_ey = -inv_before[z] * diff_z[z]
        diff_ez = inv_before[z] * diff_y[z]
        row_y = from_before(2, z) + diff_y[z] - COURANT * ((up - diff_ex[z]) - (e1_ref[2, z, first] - diff_ez))
        row_z = from_before(3, z) + diff_z[z] - COURANT * (
            (e1_ref[1, z, first] - diff_ey) - (ahead_y(diff_ex[z]) - diff_ex[z])
        )
        open_row = keep_row & has_before
        row_y = jnp.where(open_row, row_y, 0.0)
        row_z = jnp.where(open_row, row_z, 0.0)
        curl = curl_back([h2_ref[i, z] for i in range(3)], below, row_y, row_z)
        for i in range(3):
            new = k_ref[1, z] * e1_ref[i, z, :, :width] + k_ref[0, z] * curl[i][:, :width] - g_ref[i, z]
            e_out[i, z] = new
            if i < 2 and z in layers:
                store_plane(plane_ref, surface_ref, 1, layers[z], i, new)
    split_planes(plane_ref, (ev_ref, ev_low_ref, od_ref, od_low_ref), rows, pairs)


def edge_pairs(rows):
    return range(rows // 2 - 2, rows // 2)


def second_step(h1, e1, late, factors, surface, own_one, own_two, x_one, x_two):
    _, _, rows, width = late.shape
    pairs = edge_pairs(rows)
    field = jax.ShapeDtypeStruct(late.shape, jnp.float32)
    store = pltpu.VMEM(h1.shape, jnp.float32)
    return pl.pallas_call(
        partial(second_body, pairs=pairs),
        out_shape=(field, field)
        + tuple(jax.ShapeDtypeStruct(shape, jnp.bfloat16) for shape in split_shapes(pairs, width)),
        scratch_shapes=[store, store, store, pltpu.VMEM((2, 16 * rows, width // 2), jnp.float32)],
        compiler_params=VMEM,
        name="second_step",
    )(h1, e1, late, factors, surface, own_one, own_two, x_one, x_two)


def table_body(waves_ref, tie_ref, cos_ref, sin_ref, phase_ref, *, rows, width, scale):
    del tie_ref
    half = width // 2
    chunk = 256
    step = (row_index((8, chunk)).astype(jnp.float32)) + 0.5
    centre_x = (lax.axis_index("gx") * rows).astype(jnp.float32) + 0.5 * (rows - 1)
    centre_y = (lax.axis_index("gy") * width).astype(jnp.float32) + 0.5 * (width - 1)

    @pl.loop(0, waves_ref.shape[1] // chunk)
    def _(turn):
        cut = pl.ds(pl.multiple_of(turn * chunk, chunk), chunk)
        wave_x, wave_y = WAVE * waves_ref[0:1, cut], WAVE * waves_ref[1:2, cut]
        sin_x, cos_x = sincos(wave_x * step)
        phase_ref[0:8, cut] = cos_x
        phase_ref[8:16, cut] = sin_x
        sin_c, cos_c = sincos(wave_x * centre_x + wave_y * centre_y)
        phase_ref[16:24, cut] = jnp.broadcast_to(scale * cos_c, step.shape)
        phase_ref[24:32, cut] = jnp.broadcast_to(scale * sin_c, step.shape)
        sin_y, cos_y = sincos(wave_y * step)
        sin_w, cos_w = sincos(wave_y * 8.0)
        cos_y = jnp.concatenate([cos_y, cos_y * cos_w - sin_y * sin_w], axis=0)
        sin_y = jnp.concatenate([sin_y, sin_y * cos_w + cos_y[0:8] * sin_w], axis=0)
        sin_w, cos_w = 2.0 * sin_w * cos_w, 1.0 - 2.0 * sin_w * sin_w
        for start in range(0, half, 16):
            if start:
                cos_y, sin_y = cos_y * cos_w - sin_y * sin_w, sin_y * cos_w + cos_y * sin_w
            for value, ref in ((cos_y, cos_ref), (sin_y, sin_ref)):
                top = value.astype(jnp.bfloat16)
                ref[start : start + 16, cut] = top
                ref[half + start : half + start + 16, cut] = (value - top.astype(jnp.float32)).astype(jnp.bfloat16)


def tables(waves, tie, rows, width, scale):
    count = waves.shape[1]
    table = jax.ShapeDtypeStruct((width, count), jnp.bfloat16)
    return pl.pallas_call(
        partial(table_body, rows=rows, width=width, scale=scale),
        out_shape=(table, table, jax.ShapeDtypeStruct((32, count), jnp.float32)),
        in_specs=[pl.BlockSpec(memory_space=pltpu.VMEM), pl.BlockSpec(memory_space=pl.ANY)],
        compiler_params=VMEM,
        cost_estimate=pl.CostEstimate(flops=40 * width * count, bytes_accessed=4 * width * count, transcendentals=0),
        name="tables",
    )(waves, tie)


def project_body(ev_ref, ev_low_ref, od_ref, od_low_ref, cos_ref, sin_ref, phase_ref, inner_ref, out_ref, *, start, pairs):
    chunk = 256
    for at in range(0, out_ref.shape[1], chunk):
        cut, to = slice(start + at, start + at + chunk), slice(at, at + chunk)
        real, imag = project_chunk(
            (ev_ref, ev_low_ref, od_ref, od_low_ref), cos_ref, sin_ref, phase_ref, cut, pairs
        )
        out_ref[0:8, to] = real + inner_ref[0:8, cut]
        out_ref[8:16, to] = imag + inner_ref[8:16, cut]


def project(planes, cos_y, sin_y, phases, inner, rows, start, count):
    width = cos_y.shape[0]
    return pl.pallas_call(
        partial(project_body, start=start, pairs=edge_pairs(rows)),
        out_shape=jax.ShapeDtypeStruct((16, count), jnp.float32),
        compiler_params=VMEM,
        cost_estimate=pl.CostEstimate(
            flops=8 * planes[0].shape[0] * width * count, bytes_accessed=4 * width * count, transcendentals=0
        ),
        name="project",
    )(*planes, cos_y, sin_y, phases, inner)


def swap(array, axis, mask):
    return lax.ppermute(array, axis, [(i, i ^ mask) for i in range(lax.axis_size(axis))])


def swap_other(array, axis):
    pairs = [(i, ((i + 1) ^ 1) - 1) for i in range(1, lax.axis_size(axis) - 1)]
    return lax.ppermute(array, axis, pairs)


def group_of(axis):
    return min(lax.axis_size(axis), 4)


def own_first(directions):
    count_x, count_y = lax.axis_size("gx"), lax.axis_size("gy")
    group = group_of("gx")
    waves = directions.T.reshape(2, count_x // group, group, count_y // 2, 2, -1)
    place_x, place_y = lax.axis_index("gx"), lax.axis_index("gy")
    waves = jnp.where(place_y % 2 == 1, jnp.flip(waves, 4), waves)
    waves = lax.dynamic_slice_in_dim(jnp.concatenate([waves, waves], axis=2), place_x % group, group, axis=2)
    waves = exclusive(waves, 1, place_x // group)
    waves = exclusive(waves, 3, place_y // 2)
    return waves.transpose(0, 4, 1, 2, 3, 5).reshape(2, directions.shape[0])


def exclusive(array, axis, place):
    size = array.shape[axis]
    bit = 1
    while bit < size:
        pieces = jnp.split(array, size // bit, axis)
        turned = jnp.concatenate([pieces[i ^ 1] for i in range(len(pieces))], axis)
        array = jnp.where(place & bit, turned, array)
        bit = 2 * bit
    return array


def halve(far, axis, mask):
    half = far.shape[1] // 2
    return far[:, :half] + swap(far[:, half:], axis, mask)


def halve_all(far, axis, low, size):
    mask = size // 2
    while mask >= 1:
        far = halve(far, axis, mask * low)
        mask = mask // 2
    return far


def scatter_group(far, axis):
    count, group = lax.axis_size(axis), group_of(axis)
    part = far.shape[1] // group
    total = far[:, :part]
    got = []
    for step in sorted(range(1, group), key=lambda step: (step != group // 2, step)):
        pairs = [(i, i // group * group + (i + step) % group) for i in range(count)]
        got.append(lax.ppermute(far[:, step * part : (step + 1) * part], axis, pairs))
    for array in got:
        total = total + array
    return total


def local(e_field, h_field, pol_now, pol_old, eps_inf, materials, surface, poles, directions):
    _, _, rows, width = e_field.shape
    scale = 1.0 / math.sqrt(rows * lax.axis_size("gx") * width * lax.axis_size("gy"))
    one, two, near, late, factors, e_field, h_field = prepare(e_field, h_field, pol_now, pol_old, eps_inf, materials, poles)
    tie = factors
    one = swap(one, "gy", 1)
    two = swap_other(two, "gy")
    cos_y, sin_y, phases = tables(own_first(directions), tie, rows, width, scale)
    own_one, own_two, h1, e1 = first_step(e_field, h_field, near, factors, one, two, phases)
    x_one = swap(own_one, "gx", 1)
    x_two = swap_other(own_two, "gx")
    inner = inside(h1, e1, late, factors, surface, cos_y, sin_y, phases)
    e_new, h_new, *planes = second_step(h1, e1, late, factors, surface, own_one, own_two, x_one, x_two)
    half = directions.shape[0] // 2
    far = project(planes, cos_y, sin_y, phases, inner, rows, half, half)
    arrived = swap(far, "gy", 1)
    far = project(planes, cos_y, sin_y, phases, inner, rows, 0, half) + arrived
    far = halve_all(far, "gx", group_of("gx"), lax.axis_size("gx") // group_of("gx"))
    far = scatter_group(far, "gx")
    far = halve_all(far, "gy", 2, lax.axis_size("gy") // 2)
    return e_new, h_new, far.T


def solution(mesh):
    field = P("design", None, "gx", "gy")
    cell = P("design", "gx", "gy")
    return jax.shard_map(
        local,
        mesh=mesh,
        in_specs=(field, field, field, field, cell, cell, cell, P(), P()),
        out_specs=(field, field, P(("gx", "gy"), "design")),
        check_vma=False,
    )
```

```python
from functools import partial
import math

import jax
import jax.numpy as jnp
from jax import lax
from jax.experimental import pallas as pl
from jax.experimental.pallas import tpu as pltpu
from jax.sharding import PartitionSpec as P

COURANT = 0.5
WAVE = 0.3
OMEGA = 0.25
LANES = 128
GROUPS = 2
TABLE_CHUNK = 256
SLOTS = 24
VMEM = pltpu.CompilerParams(vmem_limit_bytes=24 * 1024 * 1024)


def lane_index(shape):
    return lax.broadcasted_iota(jnp.int32, shape, len(shape) - 1)


def row_index(shape):
    return lax.broadcasted_iota(jnp.int32, shape, 0)


def sincos(angle):
    turns = jnp.round(angle * (0.5 / math.pi))
    rest = angle - turns * 6.28125
    rest = rest - turns * 0.0019350051879882812
    rest = rest - turns * 3.0199159819567e-07
    half = 0.5 * rest
    sq = half * half
    sin_half = 1.0 / 6227020800.0
    for term in (-1.0 / 39916800.0, 1.0 / 362880.0, -1.0 / 5040.0, 1.0 / 120.0, -1.0 / 6.0, 1.0):
        sin_half = sin_half * sq + term
    sin_half = sin_half * half
    cos_half = -1.0 / 87178291200.0
    for term in (1.0 / 479001600.0, -1.0 / 3628800.0, 1.0 / 40320.0, -1.0 / 720.0, 1.0 / 24.0, -0.5, 1.0):
        cos_half = cos_half * sq + term
    return 2.0 * sin_half * cos_half, 1.0 - 2.0 * sin_half * sin_half


def prepare_body(e_in, h_in, p_in, q_in, eps_in, mat_in, poles_in, waves_in, one_ref, two_ref, d_ref, g_ref, k_ref,
                 e_ref, h_ref, waves_ref, p_ref, q_ref, eps_ref, mat_ref, poles_ref, table_ref, up_ref, down_ref, sems, small_sems):
    levels, rows, width = eps_ref.shape
    last = width - LANES
    pairs = ((e_in, e_ref), (h_in, h_ref), (p_in, p_ref), (q_in, q_ref), (eps_in, eps_ref), (mat_in, mat_ref))
    group = levels // GROUPS
    poles_copy = pltpu.make_async_copy(poles_in, poles_ref, small_sems.at[0])
    poles_copy.start()
    copies = []
    for part in range(GROUPS):
        cut = pl.ds(part * group, group)
        for k, (source, target) in enumerate(pairs):
            at = (slice(None), cut) if len(source.shape) == 4 else (cut,)
            copy = pltpu.make_async_copy(source.at[at], target.at[at], sems.at[part, k])
            copy.start()
            copies.append(copy)
    waves_copy = pltpu.make_async_copy(waves_in, waves_ref, small_sems.at[1])
    waves_copy.start()
    poles_copy.wait()
    table_ref[0:3, 0 : poles_ref.shape[1]] = poles_ref[...]
    omega_dt, gamma_dt, strength = (table_ref[i : i + 1, :] for i in range(3))
    denominator = 1.0 + 0.5 * gamma_dt
    tile = (rows, LANES)
    table_a = jnp.broadcast_to((2.0 - omega_dt * omega_dt) / denominator, tile)
    table_b = jnp.broadcast_to(-(1.0 - 0.5 * gamma_dt) / denominator, tile)
    table_c = jnp.broadcast_to(strength * omega_dt * omega_dt / denominator, tile)
    lane = lane_index(tile)
    even = lax.rem(lax.axis_index("gy"), 2) == 0
    for z in range(levels):
        if z % group == 0:
            for copy in copies[z // group * 6 : z // group * 6 + 6]:
                copy.wait()
        up = jnp.zeros(tile, jnp.float32)
        down = jnp.zeros(tile, jnp.float32)
        for start in range(0, width, LANES):
            cut = slice(start, start + LANES)
            number = mat_ref[z, :, cut]
            a = jnp.take_along_axis(table_a, number, axis=1)
            b = jnp.take_along_axis(table_b, number, axis=1)
            c = jnp.take_along_axis(table_c, number, axis=1)
            inv = 1.0 / eps_ref[z, :, cut]
            half = COURANT * inv
            k_ref[0, z, :, cut] = half
            k_ref[1, z, :, cut] = 1.0 - c * inv
            items = [e_ref[i, z, :, cut] for i in range(3)] + [h_ref[i, z, :, cut] for i in range(3)]
            for i in range(3):
                now, old = p_ref[i, z, :, cut], q_ref[i, z, :, cut]
                new = a * now + b * old + c * items[i]
                local = items[i] - (new - now) * inv
                d_ref[i, z, :, cut] = local
                g_ref[i, z, :, cut] = ((a * new - new) + b * now) * inv
                items.append(local)
            items.append(half)
            for k, item in enumerate(items):
                if start == 0:
                    moved = pltpu.roll(item, 2 * k, 1) if k else item
                    down = jnp.where((lane >= 2 * k) & (lane < 2 * k + 2), moved, down)
                if start == last:
                    moved = pltpu.roll(item, LANES - 2 * k, 1) if k else item
                    up = jnp.where((lane >= LANES - 2 - 2 * k) & (lane < LANES - 2 * k), moved, up)
        up_ref[z * rows : (z + 1) * rows] = up
        down_ref[z * rows : (z + 1) * rows] = down
    up = up_ref[...].T[LANES - SLOTS :]
    down = down_ref[...].T[:SLOTS]
    one_ref[...] = jnp.where(even, up, down)
    two_ref[...] = jnp.where(even, down, up)
    waves_copy.wait()


def prepare(e_field, h_field, pol_now, pol_old, eps_inf, materials, poles, waves):
    levels, rows, width = eps_inf.shape
    message = jax.ShapeDtypeStruct((SLOTS, levels * rows), jnp.float32)
    field = jax.ShapeDtypeStruct(e_field.shape, jnp.float32)
    pair = jax.ShapeDtypeStruct((2, levels, rows, width), jnp.float32)
    arrays = (e_field, h_field, pol_now, pol_old, eps_inf, materials, poles, waves)
    return pl.pallas_call(
        prepare_body,
        out_shape=(message, message, field, field, pair, field, field, jax.ShapeDtypeStruct(waves.shape, jnp.float32)),
        in_specs=[pl.BlockSpec(memory_space=pltpu.HBM)] * 8,
        scratch_shapes=[
            pltpu.VMEM(e_field.shape, jnp.float32),
            pltpu.VMEM(e_field.shape, jnp.float32),
            pltpu.VMEM(eps_inf.shape, jnp.float32),
            pltpu.VMEM(eps_inf.shape, jnp.int32),
            pltpu.VMEM(poles.shape, jnp.float32),
            pltpu.VMEM((8, LANES), jnp.float32),
            pltpu.VMEM((levels * rows, LANES), jnp.float32),
            pltpu.VMEM((levels * rows, LANES), jnp.float32),
            pltpu.SemaphoreType.DMA((GROUPS, 6)),
            pltpu.SemaphoreType.DMA((2,)),
        ],
        compiler_params=VMEM,
        name="prepare",
    )(*(pltpu.with_memory_space_constraint(array, pltpu.HBM) for array in arrays))


def read_wide(own_ref, index, z, halo_ref, item):
    both = halo_ref[z]
    lane = lane_index(both.shape)
    shift = 2 * item
    late = pltpu.roll(both, LANES - shift, 1) if item else both
    early = pltpu.roll(both, shift, 1) if item else both
    halo = jnp.where(lane < 2, late, jnp.where(lane >= LANES - 2, early, 0.0))
    return jnp.concatenate([own_ref[index, z], halo], axis=1)


def read_y_messages(one_ref, two_ref, halo_ref):
    place = lax.axis_index("gy")
    even = lax.rem(place, 2) == 0
    one, two = one_ref[...], two_ref[...]
    before = jnp.where(place > 0, jnp.where(even, two, one), 0.0)
    after = jnp.where(place < lax.axis_size("gy") - 1, jnp.where(even, one, two), 0.0)
    blank = jnp.zeros((LANES - 2 * SLOTS, one.shape[1]), jnp.float32)
    halo_ref[...] = jnp.concatenate([after, blank, before], axis=0).T.reshape(halo_ref.shape)


def ahead_y(v):
    return pltpu.roll(v, v.shape[1] - 1, 1)


def behind_y(v):
    return pltpu.roll(v, 1, 1)


def ahead_x(v, row):
    at = row_index(v.shape)
    return jnp.where(at == v.shape[0] - 1, row, pltpu.roll(v, v.shape[0] - 1, 0))


def behind_x(v, row):
    at = row_index(v.shape)
    return jnp.where(at == 0, row, pltpu.roll(v, 1, 0))


def magnetic(e_here, e_above, h_here, row_y, row_z, keep):
    ex, ey, ez = e_here
    hx, hy, hz = h_here
    up_x, up_y = e_above
    hx = hx - COURANT * ((ahead_y(ez) - ez) - (up_y - ey))
    hy = hy - COURANT * ((up_x - ex) - (ahead_x(ez, row_z) - ez))
    hz = hz - COURANT * ((ahead_x(ey, row_y) - ey) - (ahead_y(ex) - ex))
    return [jnp.where(keep, v, 0.0) for v in (hx, hy, hz)]


def curl_back(h_here, h_below, row_y, row_z):
    hx, hy, hz = h_here
    low_x, low_y = h_below
    return (
        (hz - behind_y(hz)) - (hy - low_y),
        (hx - low_x) - (hz - behind_x(hz, row_z)),
        (hy - behind_x(hy, row_y)) - (hx - behind_y(hx)),
    )


def kept_lanes(shape, width):
    return (lane_index(shape) < width + LANES // 2) | (lax.axis_index("gy") > 0)


def first_body(e_ref, h_ref, d_ref, k_ref, one_ref, two_ref, tie_ref, out_one_ref, out_two_ref, h1_ref, e1_ref, e0_ref, halo_ref):
    del tie_ref
    _, levels, rows, width = e_ref.shape
    wide = (rows, width + LANES)
    read_y_messages(one_ref, two_ref, halo_ref)
    keep = kept_lanes(wide, width)
    zero_row = jnp.zeros((1, wide[1]), jnp.float32)
    zero = jnp.zeros(wide, jnp.float32)
    for z in range(levels):
        for i in range(3):
            e0_ref[i, z] = read_wide(e_ref, i, z, halo_ref, i)
    for z in range(levels):
        above = [e0_ref[i, z + 1] for i in range(2)] if z + 1 < levels else [zero, zero]
        h_here = [read_wide(h_ref, i, z, halo_ref, 3 + i) for i in range(3)]
        new = magnetic([e0_ref[i, z] for i in range(3)], above, h_here, zero_row, zero_row, keep)
        for i in range(3):
            h1_ref[i, z] = new[i]
    inv = []
    for z in range(levels):
        below = [h1_ref[i, z - 1] for i in range(2)] if z else [zero, zero]
        curl = curl_back([h1_ref[i, z] for i in range(3)], below, zero_row, zero_row)
        inv.append(read_wide(k_ref, 0, z, halo_ref, 9))
        for i in range(3):
            e1_ref[i, z] = read_wide(d_ref, i, z, halo_ref, 6 + i) + inv[z] * curl[i]
    even = lax.rem(lax.axis_index("gx"), 2) == 0
    keep_row = kept_lanes((1, wide[1]), width)
    end = slice(rows - 1, rows)
    for z in range(levels):
        hy, hz = h1_ref[1, z, end], h1_ref[2, z, end]
        ex, ey, ez = (e1_ref[i, z, end] for i in range(3))
        up_x = e1_ref[0, z + 1, end] if z + 1 < levels else zero_row
        second_y = hy - COURANT * ((up_x - ex) + ez)
        second_z = hz - COURANT * (-ey - (ahead_y(ex) - ex))
        up = [hy, hz, jnp.where(keep_row, second_y, 0.0), jnp.where(keep_row, second_z, 0.0), inv[z][end]]
        down = [e0_ref[1, z, 0:1], e0_ref[2, z, 0:1], e1_ref[1, z, 0:1], e1_ref[2, z, 0:1], inv[z][0:1]]
        for k in range(5):
            out_one_ref[k, z : z + 1] = jnp.where(even, up[k], down[k])
            out_two_ref[k, z : z + 1] = jnp.where(even, down[k], up[k])


def first_step(e_field, h_field, local, factors, one, two, tie):
    _, levels, rows, width = e_field.shape
    message = jax.ShapeDtypeStruct((5, levels, width + LANES), jnp.float32)
    store = (3, levels, rows, width + LANES)
    field = jax.ShapeDtypeStruct(store, jnp.float32)
    vmem = pl.BlockSpec(memory_space=pltpu.VMEM)
    return pl.pallas_call(
        first_body,
        out_shape=(message, message, field, field),
        in_specs=[vmem] * 6 + [pl.BlockSpec(memory_space=pl.ANY)],
        scratch_shapes=[pltpu.VMEM(store, jnp.float32), pltpu.VMEM((levels, rows, LANES), jnp.float32)],
        compiler_params=VMEM,
        name="first_step",
    )(e_field, h_field, local, factors, one, two, tie)


def store_plane(plane_ref, surface_ref, number, layer, part, value):
    rows, half = value.shape[0], plane_ref.shape[2]
    at = ((number * 2 + layer) * 4 + part) * rows
    weighted = value[:, : 2 * half] * surface_ref[layer].astype(jnp.float32)
    plane_ref[0, at : at + rows] = weighted[:, :half]
    plane_ref[1, at : at + rows] = weighted[:, half:]


def split_planes(plane_ref, split_refs, rows, pairs):
    kinds = 16
    half = plane_ref.shape[2]
    count = split_refs[0].shape[0] // 2
    back = half - 1 - lane_index((kinds, half))
    for turn, v in enumerate(pairs):
        high = [plane_ref[side, pl.ds(rows // 2 + v, kinds, stride=rows), :] for side in range(2)]
        low = [plane_ref[side, pl.ds(rows // 2 - 1 - v, kinds, stride=rows), :] for side in range(2)]
        for parity in range(2):
            left, right = (b - a if parity else b + a for a, b in zip(low, high))
            left = jnp.take_along_axis(left, back, axis=1)
            at = slice((2 * turn + parity) * kinds, (2 * turn + parity + 1) * kinds)
            below = slice(count + at.start, count + at.stop)
            for value, ref in zip((right + left, right - left), split_refs):
                top = value.astype(jnp.bfloat16)
                ref[at, :half] = top
                ref[at, half:] = top
                ref[below, :half] = (value - top.astype(jnp.float32)).astype(jnp.bfloat16)
                ref[below, half:] = jnp.zeros_like(top)


def project_chunk(split_refs, cos_ref, sin_ref, phase_ref, cut, pairs):
    even_ref, odd_ref = split_refs
    count = even_ref.shape[0] // 2
    part_c = jnp.dot(even_ref[...], cos_ref[:, cut], preferred_element_type=jnp.float32)
    part_s = jnp.dot(odd_ref[...], sin_ref[:, cut], preferred_element_type=jnp.float32)
    part_c = part_c[:count] + part_c[count:]
    part_s = part_s[:count] + part_s[count:]
    real = [0.0, 0.0]
    imag = [0.0, 0.0]
    for turn, v in enumerate(pairs):
        cos_x = phase_ref[v : v + 1, cut]
        sin_x = phase_ref[8 + v : 9 + v, cut]
        for n in range(2):
            same = slice((turn * 4 + n) * 8, (turn * 4 + n) * 8 + 8)
            flip = slice((turn * 4 + 2 + n) * 8, (turn * 4 + 2 + n) * 8 + 8)
            real[n] = real[n] + (cos_x * part_c[same] - sin_x * part_s[flip])
            imag[n] = imag[n] + (cos_x * part_s[same] + sin_x * part_c[flip])
    sum_real = 0.0
    sum_imag = 0.0
    for n in range(2):
        cos_n, sin_n = math.cos(OMEGA * (n + 1)), math.sin(OMEGA * (n + 1))
        sum_real = sum_real + (cos_n * real[n] + sin_n * imag[n])
        sum_imag = sum_imag + (cos_n * imag[n] - sin_n * real[n])
    cos_c, sin_c = phase_ref[16:24, cut], phase_ref[24:32, cut]
    return sum_real * cos_c - sum_imag * sin_c, sum_real * sin_c + sum_imag * cos_c


def split_shapes(pairs, width):
    return [(2 * 32 * len(pairs), width)] * 2


def inside_body(h1_ref, e1_ref, g_ref, k_ref, surface_ref, cos_ref, sin_ref, phase_ref, out_ref, plane_ref, *split_refs, pairs):
    _, levels, rows, _ = h1_ref.shape
    width = g_ref.shape[3]
    wide = (rows, h1_ref.shape[3])
    keep = kept_lanes(wide, width)
    zero_row = jnp.zeros((1, wide[1]), jnp.float32)
    zero = jnp.zeros(wide, jnp.float32)

    def second(z):
        above = [e1_ref[i, z + 1] for i in range(2)] if z + 1 < levels else [zero, zero]
        here = [e1_ref[i, z] for i in range(3)]
        return magnetic(here, above, [h1_ref[i, z] for i in range(3)], zero_row, zero_row, keep)

    for layer, z in enumerate((0, levels - 1)):
        h2 = second(z)
        below = second(z - 1)[:2] if z else [zero, zero]
        curl = curl_back(h2, below, zero_row, zero_row)
        for i in range(2):
            store_plane(plane_ref, surface_ref, 0, layer, i, e1_ref[i, z])
            store_plane(plane_ref, surface_ref, 0, layer, 2 + i, h1_ref[i, z])
            new = k_ref[1, z] * e1_ref[i, z, :, :width] + k_ref[0, z] * curl[i][:, :width] - g_ref[i, z]
            store_plane(plane_ref, surface_ref, 1, layer, i, new)
            store_plane(plane_ref, surface_ref, 1, layer, 2 + i, h2[i])
    split_planes(plane_ref, split_refs, rows, pairs)
    chunk = 256
    for at in range(0, out_ref.shape[1], chunk):
        cut = slice(at, at + chunk)
        out_ref[0:8, cut], out_ref[8:16, cut] = project_chunk(split_refs, cos_ref, sin_ref, phase_ref, cut, pairs)


def inside(h1, e1, late, factors, surface, cos_y, sin_y, phases):
    _, _, rows, width = late.shape
    pairs = range(rows // 2 - 2)
    count = cos_y.shape[1]
    return pl.pallas_call(
        partial(inside_body, pairs=pairs),
        out_shape=jax.ShapeDtypeStruct((16, count), jnp.float32),
        scratch_shapes=[pltpu.VMEM((2, 16 * rows, width // 2), jnp.float32)]
        + [pltpu.VMEM(shape, jnp.bfloat16) for shape in split_shapes(pairs, width)],
        compiler_params=VMEM,
        cost_estimate=pl.CostEstimate(
            flops=8 * 32 * len(pairs) * width * count, bytes_accessed=4 * width * count, transcendentals=0
        ),
        name="inside",
    )(h1, e1, late, factors, surface, cos_y, sin_y, phases)


def second_body(h1_in, e1_in, g_ref, k_ref, surface_ref, own_one_ref, own_two_ref, x_one_ref, x_two_ref, e_out, h_out,
                even_ref, odd_ref, h1_ref, e1_ref, h2_ref, plane_ref, *, pairs):
    _, levels, rows, _ = h1_in.shape
    width = g_ref.shape[3]
    wide = (rows, h1_in.shape[3])
    keep = kept_lanes(wide, width)
    keep_row = kept_lanes((1, wide[1]), width)
    zero_row = jnp.zeros((1, wide[1]), jnp.float32)
    zero = jnp.zeros(wide, jnp.float32)
    at_row = row_index(wide)
    place, count = lax.axis_index("gx"), lax.axis_size("gx")
    even = lax.rem(place, 2) == 0
    has_before, has_after = place > 0, place < count - 1
    first, end = slice(0, 1), slice(rows - 1, rows)
    layers = {0: 0, levels - 1: 1}

    def from_before(k, z):
        got = jnp.where(even, x_two_ref[k, z : z + 1], x_one_ref[k, z : z + 1])
        return jnp.where(has_before, got, 0.0)

    def from_after(k, z):
        got = jnp.where(even, x_one_ref[k, z : z + 1], x_two_ref[k, z : z + 1])
        return jnp.where(has_after, got, 0.0)

    def own_up(k, z):
        return jnp.where(even, own_one_ref[k, z : z + 1], own_two_ref[k, z : z + 1])

    def own_down(k, z):
        return jnp.where(even, own_two_ref[k, z : z + 1], own_one_ref[k, z : z + 1])

    def patched(value, start, stop):
        if start is not None:
            value = jnp.where(at_row == 0, value + start, value)
        return jnp.where(at_row == rows - 1, value + stop, value)

    diff_y = [jnp.where(has_before, COURANT * own_down(1, z), 0.0) for z in range(levels)]
    diff_z = [jnp.where(has_before, -COURANT * own_down(0, z), 0.0) for z in range(levels)]
    last_y = [COURANT * from_after(1, z) for z in range(levels)]
    last_z = [-COURANT * from_after(0, z) for z in range(levels)]
    for z in range(levels):
        h1 = [h1_in[0, z], patched(h1_in[1, z], None, last_y[z]), patched(h1_in[2, z], None, last_z[z])]
        low = last_y[z - 1] if z else zero_row
        inv, inv_first = own_up(4, z), own_down(4, z)
        stop_x = inv * ((last_z[z] - behind_y(last_z[z])) - (last_y[z] - low))
        start_y = inv_first * (from_before(1, z) + diff_z[z])
        start_z = -inv_first * (from_before(0, z) + diff_y[z])
        e1 = [
            patched(e1_in[0, z], None, stop_x),
            patched(e1_in[1, z], start_y, -inv * last_z[z]),
            patched(e1_in[2, z], start_z, inv * last_y[z]),
        ]
        for i in range(3):
            h1_ref[i, z] = h1[i]
            e1_ref[i, z] = e1[i]
        if z in layers:
            for i in range(2):
                store_plane(plane_ref, surface_ref, 0, layers[z], i, e1[i])
                store_plane(plane_ref, surface_ref, 0, layers[z], 2 + i, h1[i])

    for z in range(levels):
        above = [e1_ref[i, z + 1] for i in range(2)] if z + 1 < levels else [zero, zero]
        inv = from_after(4, z)
        row_y = from_after(2, z) + inv * h1_ref[2, z, end]
        row_z = from_after(3, z) - inv * h1_ref[1, z, end]
        new = magnetic(
            [e1_ref[i, z] for i in range(3)], above, [h1_ref[i, z] for i in range(3)], row_y, row_z, keep
        )
        for i in range(3):
            h2_ref[i, z] = new[i]
            h_out[i, z] = new[i][:, :width]
        if z in layers:
            for i in range(2):
                store_plane(plane_ref, surface_ref, 1, layers[z], 2 + i, new[i])

    inv_before = [from_before(4, z) for z in range(levels)]
    diff_ex = []
    for z in range(levels):
        low = diff_y[z - 1] if z else zero_row
        diff_ex.append(inv_before[z] * ((diff_z[z] - behind_y(diff_z[z])) - (diff_y[z] - low)))
    for z in range(levels):
        below = [h2_ref[i, z - 1] for i in range(2)] if z else [zero, zero]
        up = diff_ex[z + 1] if z + 1 < levels else zero_row
        diff_ey = -inv_before[z] * diff_z[z]
        diff_ez = inv_before[z] * diff_y[z]
        row_y = from_before(2, z) + diff_y[z] - COURANT * ((up - diff_ex[z]) - (e1_ref[2, z, first] - diff_ez))
        row_z = from_before(3, z) + diff_z[z] - COURANT * (
            (e1_ref[1, z, first] - diff_ey) - (ahead_y(diff_ex[z]) - diff_ex[z])
        )
        open_row = keep_row & has_before
        row_y = jnp.where(open_row, row_y, 0.0)
        row_z = jnp.where(open_row, row_z, 0.0)
        curl = curl_back([h2_ref[i, z] for i in range(3)], below, row_y, row_z)
        for i in range(3):
            new = k_ref[1, z] * e1_ref[i, z, :, :width] + k_ref[0, z] * curl[i][:, :width] - g_ref[i, z]
            e_out[i, z] = new
            if i < 2 and z in layers:
                store_plane(plane_ref, surface_ref, 1, layers[z], i, new)
    split_planes(plane_ref, (even_ref, odd_ref), rows, pairs)


def edge_pairs(rows):
    return range(rows // 2 - 2, rows // 2)


def second_step(h1, e1, late, factors, surface, own_one, own_two, x_one, x_two):
    _, _, rows, width = late.shape
    pairs = edge_pairs(rows)
    field = jax.ShapeDtypeStruct(late.shape, jnp.float32)
    store = pltpu.VMEM(h1.shape, jnp.float32)
    return pl.pallas_call(
        partial(second_body, pairs=pairs),
        out_shape=(pltpu.VMEM(late.shape, jnp.float32), pltpu.VMEM(late.shape, jnp.float32))
        + tuple(jax.ShapeDtypeStruct(shape, jnp.bfloat16) for shape in split_shapes(pairs, width)),
        scratch_shapes=[store, store, store, pltpu.VMEM((2, 16 * rows, width // 2), jnp.float32)],
        compiler_params=VMEM,
        name="second_step",
    )(h1, e1, late, factors, surface, own_one, own_two, x_one, x_two)


def table_body(waves_ref, cos_ref, sin_ref, phase_ref, centre_ref, *, rows, width, scale, owned):
    half = width // 2
    chunk = TABLE_CHUNK
    chunks = waves_ref.shape[1] // chunk
    step = (row_index((8, chunk)).astype(jnp.float32)) + 0.5
    centre_x = (lax.axis_index("gx") * rows).astype(jnp.float32) + 0.5 * (rows - 1)
    centre_y = (lax.axis_index("gy") * width).astype(jnp.float32) + 0.5 * (width - 1)
    for k in range(chunks):
        cut = slice(k * chunk, (k + 1) * chunk)
        centre_ref[0, k : k + 1] = WAVE * waves_ref[0:1, cut] * centre_x + WAVE * waves_ref[1:2, cut] * centre_y
    sin_c, cos_c = sincos(centre_ref[0])
    centre_ref[0] = scale * cos_c
    centre_ref[1] = scale * sin_c

    @pl.loop(0, chunks, unroll=2)
    def _(turn):
        cut = pl.ds(pl.multiple_of(turn * chunk, chunk), chunk)
        source = block_source(turn, owned // chunk) if owned % chunk == 0 else turn
        at = pl.ds(pl.multiple_of(source * chunk, chunk), chunk)
        wave_x, wave_y = WAVE * waves_ref[0:1, at], WAVE * waves_ref[1:2, at]
        sin_x, cos_x = sincos(wave_x * step)
        phase_ref[0:8, cut] = cos_x
        phase_ref[8:16, cut] = sin_x
        phase_ref[16:24, cut] = jnp.broadcast_to(centre_ref[0, pl.ds(source, 1)], step.shape)
        phase_ref[24:32, cut] = jnp.broadcast_to(centre_ref[1, pl.ds(source, 1)], step.shape)
        sin_y, cos_y = sincos(wave_y * step)
        cos_w = cos_y[7:8] * cos_y[0:1] - sin_y[7:8] * sin_y[0:1]
        sin_w = sin_y[7:8] * cos_y[0:1] + cos_y[7:8] * sin_y[0:1]
        next_cos = cos_y * cos_w - sin_y * sin_w
        next_sin = sin_y * cos_w + cos_y * sin_w
        cos_y = jnp.concatenate([cos_y, next_cos], axis=0)
        sin_y = jnp.concatenate([sin_y, next_sin], axis=0)
        sin_w, cos_w = 2.0 * sin_w * cos_w, 1.0 - 2.0 * sin_w * sin_w
        for start in range(0, half, 16):
            if start:
                cos_y, sin_y = cos_y * cos_w - sin_y * sin_w, sin_y * cos_w + cos_y * sin_w
            for value, ref in ((cos_y, cos_ref), (sin_y, sin_ref)):
                top = value.astype(jnp.bfloat16)
                ref[start : start + 16, cut] = top
                ref[half + start : half + start + 16, cut] = (value - top.astype(jnp.float32)).astype(jnp.bfloat16)


def block_source(block, each):
    count_x, count_y = lax.axis_size("gx"), lax.axis_size("gy")
    group = group_of("gx")
    place_x, place_y = lax.axis_index("gx"), lax.axis_index("gy")
    rest, within = block // each, block % each
    rest, far_y = rest // (count_y // 2), rest % (count_y // 2)
    rest, near_x = rest // group, rest % group
    core, far_x = rest // (count_x // group), rest % (count_x // group)
    owner_x = (far_x ^ (place_x // group)) * group + (place_x + near_x) % group
    owner_y = (far_y ^ (place_y // 2)) * 2 + (core ^ (place_y % 2))
    return (owner_x * count_y + owner_y) * each + within


def tables(waves, rows, width, scale):
    count = waves.shape[1]
    owned = count // (lax.axis_size("gx") * lax.axis_size("gy"))
    table = jax.ShapeDtypeStruct((width, count), jnp.bfloat16)
    return pl.pallas_call(
        partial(table_body, rows=rows, width=width, scale=scale, owned=owned),
        out_shape=(table, table, jax.ShapeDtypeStruct((32, count), jnp.float32)),
        scratch_shapes=[pltpu.VMEM((2, count // TABLE_CHUNK, TABLE_CHUNK), jnp.float32)],
        compiler_params=VMEM,
        cost_estimate=pl.CostEstimate(flops=40 * width * count, bytes_accessed=4 * width * count, transcendentals=0),
        name="tables",
    )(waves)


def project_body(even_ref, odd_ref, cos_ref, sin_ref, phase_ref, inner_ref, out_ref, *, start, pairs):
    chunk = 256
    for at in range(0, out_ref.shape[1], chunk):
        cut, to = slice(start + at, start + at + chunk), slice(at, at + chunk)
        real, imag = project_chunk((even_ref, odd_ref), cos_ref, sin_ref, phase_ref, cut, pairs)
        out_ref[0:8, to] = real + inner_ref[0:8, cut]
        out_ref[8:16, to] = imag + inner_ref[8:16, cut]


def project(planes, cos_y, sin_y, phases, inner, rows, start, count):
    width = cos_y.shape[0]
    return pl.pallas_call(
        partial(project_body, start=start, pairs=edge_pairs(rows)),
        out_shape=jax.ShapeDtypeStruct((16, count), jnp.float32),
        compiler_params=VMEM,
        cost_estimate=pl.CostEstimate(
            flops=8 * planes[0].shape[0] * width * count, bytes_accessed=4 * width * count, transcendentals=0
        ),
        name="project",
    )(*planes, cos_y, sin_y, phases, inner)


def swap(array, axis, mask):
    return lax.ppermute(array, axis, [(i, i ^ mask) for i in range(lax.axis_size(axis))])


def swap_other(array, axis):
    pairs = [(i, ((i + 1) ^ 1) - 1) for i in range(1, lax.axis_size(axis) - 1)]
    return lax.ppermute(array, axis, pairs)


def group_of(axis):
    return min(lax.axis_size(axis), 4)


def own_first(directions):
    count_x, count_y = lax.axis_size("gx"), lax.axis_size("gy")
    group = group_of("gx")
    waves = directions.T.reshape(2, count_x // group, group, count_y // 2, 2, -1)
    place_x, place_y = lax.axis_index("gx"), lax.axis_index("gy")
    waves = jnp.where(place_y % 2 == 1, jnp.flip(waves, 4), waves)
    waves = lax.dynamic_slice_in_dim(jnp.concatenate([waves, waves], axis=2), place_x % group, group, axis=2)
    waves = exclusive(waves, 1, place_x // group)
    waves = exclusive(waves, 3, place_y // 2)
    return waves.transpose(0, 4, 1, 2, 3, 5).reshape(2, directions.shape[0])


def exclusive(array, axis, place):
    size = array.shape[axis]
    bit = 1
    while bit < size:
        pieces = jnp.split(array, size // bit, axis)
        turned = jnp.concatenate([pieces[i ^ 1] for i in range(len(pieces))], axis)
        array = jnp.where(place & bit, turned, array)
        bit = 2 * bit
    return array


def halve(far, axis, mask):
    half = far.shape[1] // 2
    return far[:, :half] + swap(far[:, half:], axis, mask)


def halve_all(far, axis, low, size):
    mask = size // 2
    while mask >= 1:
        far = halve(far, axis, mask * low)
        mask = mask // 2
    return far


def scatter_group(far, axis):
    count, group = lax.axis_size(axis), group_of(axis)
    part = far.shape[1] // group
    total = far[:, :part]
    got = []
    for step in sorted(range(1, group), key=lambda step: (step != group // 2, step)):
        pairs = [(i, i // group * group + (i + step) % group) for i in range(count)]
        got.append(lax.ppermute(far[:, step * part : (step + 1) * part], axis, pairs))
    for array in got:
        total = total + array
    return total


def local(e_field, h_field, pol_now, pol_old, eps_inf, materials, surface, poles, directions):
    _, _, rows, width = e_field.shape
    scale = 1.0 / math.sqrt(rows * lax.axis_size("gx") * width * lax.axis_size("gy"))
    owned = directions.shape[0] // (lax.axis_size("gx") * lax.axis_size("gy"))
    waves = directions.T if owned % TABLE_CHUNK == 0 else own_first(directions)
    one, two, near, late, factors, e_field, h_field, waves = prepare(
        e_field, h_field, pol_now, pol_old, eps_inf, materials, poles, waves
    )
    one = swap(one, "gy", 1)
    two = swap_other(two, "gy")
    cos_y, sin_y, phases = tables(waves, rows, width, scale)
    own_one, own_two, h1, e1 = first_step(e_field, h_field, near, factors, one, two, phases)
    x_one = swap(own_one, "gx", 1)
    x_two = swap_other(own_two, "gx")
    inner = inside(h1, e1, late, factors, surface, cos_y, sin_y, phases)
    e_new, h_new, *planes = second_step(h1, e1, late, factors, surface, own_one, own_two, x_one, x_two)
    half = directions.shape[0] // 2
    far = project(planes, cos_y, sin_y, phases, inner, rows, half, half)
    arrived = swap(far, "gy", 1)
    far = project(planes, cos_y, sin_y, phases, inner, rows, 0, half) + arrived
    far = halve_all(far, "gx", group_of("gx"), lax.axis_size("gx") // group_of("gx"))
    far = scatter_group(far, "gx")
    far = halve_all(far, "gy", 2, lax.axis_size("gy") // 2)
    return e_new, h_new, far.T


def solution(mesh):
    field = P("design", None, "gx", "gy")
    cell = P("design", "gx", "gy")
    return jax.shard_map(
        local,
        mesh=mesh,
        in_specs=(field, field, field, field, cell, cell, cell, P(), P()),
        out_specs=(field, field, P(("gx", "gy"), "design")),
        check_vma=False,
    )
```

```python
from functools import partial
import math

import jax
import jax.numpy as jnp
from jax import lax
from jax.experimental import pallas as pl
from jax.experimental.pallas import tpu as pltpu
from jax.sharding import PartitionSpec as P

COURANT = 0.5
WAVE = 0.3
OMEGA = 0.25
LANES = 128
GROUPS = 2
TABLE_CHUNK = 256
SLOT = 40
PACKED = LANES // SLOT
VMEM = pltpu.CompilerParams(vmem_limit_bytes=24 * 1024 * 1024)


def lane_index(shape):
    return lax.broadcasted_iota(jnp.int32, shape, len(shape) - 1)


def row_index(shape):
    return lax.broadcasted_iota(jnp.int32, shape, 0)


def sincos(angle):
    turns = jnp.round(angle * (0.5 / math.pi))
    rest = angle - turns * 6.28125
    rest = rest - turns * 0.0019350051879882812
    rest = rest - turns * 3.0199159819567e-07
    half = 0.5 * rest
    sq = half * half
    sin_half = 1.0 / 6227020800.0
    for term in (-1.0 / 39916800.0, 1.0 / 362880.0, -1.0 / 5040.0, 1.0 / 120.0, -1.0 / 6.0, 1.0):
        sin_half = sin_half * sq + term
    sin_half = sin_half * half
    cos_half = -1.0 / 87178291200.0
    for term in (1.0 / 479001600.0, -1.0 / 3628800.0, 1.0 / 40320.0, -1.0 / 720.0, 1.0 / 24.0, -0.5, 1.0):
        cos_half = cos_half * sq + term
    return 2.0 * sin_half * cos_half, 1.0 - 2.0 * sin_half * sin_half


def prepare_body(e_in, h_in, p_in, q_in, eps_in, mat_in, poles_in, waves_in, message_ref, d_ref, g_ref, k_ref,
                 e_ref, h_ref, waves_ref, p_ref, q_ref, eps_ref, mat_ref, poles_ref, table_ref, sems, small_sems):
    levels, rows, width = eps_ref.shape
    last = width - LANES
    pairs = ((e_in, e_ref), (h_in, h_ref), (p_in, p_ref), (q_in, q_ref), (eps_in, eps_ref), (mat_in, mat_ref))
    group = levels // GROUPS
    poles_copy = pltpu.make_async_copy(poles_in, poles_ref, small_sems.at[0])
    poles_copy.start()
    copies = []
    for part in range(GROUPS):
        cut = pl.ds(part * group, group)
        for k, (source, target) in enumerate(pairs):
            at = (slice(None), cut) if len(source.shape) == 4 else (cut,)
            copy = pltpu.make_async_copy(source.at[at], target.at[at], sems.at[part, k])
            copy.start()
            copies.append(copy)
    waves_copy = pltpu.make_async_copy(waves_in, waves_ref, small_sems.at[1])
    waves_copy.start()
    poles_copy.wait()
    table_ref[0:3, 0 : poles_ref.shape[1]] = poles_ref[...]
    omega_dt, gamma_dt, strength = (table_ref[i : i + 1, :] for i in range(3))
    denominator = 1.0 + 0.5 * gamma_dt
    tile = (rows, LANES)
    table_a = jnp.broadcast_to((2.0 - omega_dt * omega_dt) / denominator, tile)
    table_b = jnp.broadcast_to(-(1.0 - 0.5 * gamma_dt) / denominator, tile)
    table_c = jnp.broadcast_to(strength * omega_dt * omega_dt / denominator, tile)
    lane = lane_index(tile)
    for z in range(levels):
        if z % group == 0:
            for copy in copies[z // group * 6 : z // group * 6 + 6]:
                copy.wait()
        if z % PACKED == 0:
            message = jnp.zeros(tile, jnp.float32)
        base = z % PACKED * SLOT
        edges = []
        for start in range(0, width, LANES):
            cut = slice(start, start + LANES)
            number = mat_ref[z, :, cut]
            a = jnp.take_along_axis(table_a, number, axis=1)
            b = jnp.take_along_axis(table_b, number, axis=1)
            c = jnp.take_along_axis(table_c, number, axis=1)
            inv = 1.0 / eps_ref[z, :, cut]
            half = COURANT * inv
            k_ref[0, z, :, cut] = half
            k_ref[1, z, :, cut] = 1.0 - c * inv
            items = [e_ref[i, z, :, cut] for i in range(3)] + [h_ref[i, z, :, cut] for i in range(3)]
            for i in range(3):
                now, old = p_ref[i, z, :, cut], q_ref[i, z, :, cut]
                new = a * now + b * old + c * items[i]
                local = items[i] - (new - now) * inv
                d_ref[i, z, :, cut] = local
                g_ref[i, z, :, cut] = ((a * new - new) + b * now) * inv
                items.append(local)
            items.append(half)
            if start in (0, last):
                edges.append(items)
        for k, (left, right) in enumerate(zip(edges[0], edges[-1])):
            at = base + 4 * k
            item = pltpu.roll(jnp.where(lane < 2, left, right), at + 2, 1)
            message = jnp.where((lane >= at) & (lane < at + 4), item, message)
        if z % PACKED == PACKED - 1 or z == levels - 1:
            message_ref[z // PACKED] = message
    waves_copy.wait()


def prepare(e_field, h_field, pol_now, pol_old, eps_inf, materials, poles, waves):
    levels, rows, width = eps_inf.shape
    message = jax.ShapeDtypeStruct((-(-levels // PACKED), rows, LANES), jnp.float32)
    field = jax.ShapeDtypeStruct(e_field.shape, jnp.float32)
    pair = jax.ShapeDtypeStruct((2, levels, rows, width), jnp.float32)
    arrays = (e_field, h_field, pol_now, pol_old, eps_inf, materials, poles, waves)
    return pl.pallas_call(
        prepare_body,
        out_shape=(message, field, field, pair, field, field, jax.ShapeDtypeStruct(waves.shape, jnp.float32)),
        in_specs=[pl.BlockSpec(memory_space=pltpu.HBM)] * 8,
        scratch_shapes=[
            pltpu.VMEM(e_field.shape, jnp.float32),
            pltpu.VMEM(e_field.shape, jnp.float32),
            pltpu.VMEM(eps_inf.shape, jnp.float32),
            pltpu.VMEM(eps_inf.shape, jnp.int32),
            pltpu.VMEM(poles.shape, jnp.float32),
            pltpu.VMEM((8, LANES), jnp.float32),
            pltpu.SemaphoreType.DMA((GROUPS, 6)),
            pltpu.SemaphoreType.DMA((2,)),
        ],
        compiler_params=VMEM,
        name="prepare",
    )(*(pltpu.with_memory_space_constraint(array, pltpu.HBM) for array in arrays))


def read_wide(own_ref, index, z, messages, item):
    both = messages[z // PACKED]
    lane = lane_index(both.shape)
    both = pltpu.roll(both, LANES - 2 - (z % PACKED * SLOT + 4 * item), 1)
    halo = jnp.where((lane < 2) | (lane >= LANES - 2), both, 0.0)
    return jnp.concatenate([own_ref[index, z], halo], axis=1)


def read_y_messages(one_ref, two_ref):
    place = lax.axis_index("gy")
    even = lax.rem(place, 2) == 0
    messages = []
    for k in range(one_ref.shape[0]):
        one, two = one_ref[k], two_ref[k]
        before = jnp.where(place > 0, jnp.where(even, two, one), 0.0)
        after = jnp.where(place < lax.axis_size("gy") - 1, jnp.where(even, one, two), 0.0)
        messages.append(jnp.where(lane_index(one.shape) % 4 < 2, before, after))
    return messages


def ahead_y(v):
    return pltpu.roll(v, v.shape[1] - 1, 1)


def behind_y(v):
    return pltpu.roll(v, 1, 1)


def ahead_x(v, row):
    at = row_index(v.shape)
    return jnp.where(at == v.shape[0] - 1, row, pltpu.roll(v, v.shape[0] - 1, 0))


def behind_x(v, row):
    at = row_index(v.shape)
    return jnp.where(at == 0, row, pltpu.roll(v, 1, 0))


def magnetic(e_here, e_above, h_here, row_y, row_z, keep):
    ex, ey, ez = e_here
    hx, hy, hz = h_here
    up_x, up_y = e_above
    hx = hx - COURANT * ((ahead_y(ez) - ez) - (up_y - ey))
    hy = hy - COURANT * ((up_x - ex) - (ahead_x(ez, row_z) - ez))
    hz = hz - COURANT * ((ahead_x(ey, row_y) - ey) - (ahead_y(ex) - ex))
    return [jnp.where(keep, v, 0.0) for v in (hx, hy, hz)]


def curl_back(h_here, h_below, row_y, row_z):
    hx, hy, hz = h_here
    low_x, low_y = h_below
    return (
        (hz - behind_y(hz)) - (hy - low_y),
        (hx - low_x) - (hz - behind_x(hz, row_z)),
        (hy - behind_x(hy, row_y)) - (hx - behind_y(hx)),
    )


def kept_lanes(shape, width):
    return (lane_index(shape) < width + LANES // 2) | (lax.axis_index("gy") > 0)


def first_body(e_ref, h_ref, d_ref, k_ref, one_ref, two_ref, tie_ref, out_one_ref, out_two_ref, h1_ref, e1_ref, e0_ref):
    del tie_ref
    _, levels, rows, width = e_ref.shape
    wide = (rows, width + LANES)
    messages = read_y_messages(one_ref, two_ref)
    keep = kept_lanes(wide, width)
    zero_row = jnp.zeros((1, wide[1]), jnp.float32)
    zero = jnp.zeros(wide, jnp.float32)
    for z in range(levels):
        for i in range(3):
            e0_ref[i, z] = read_wide(e_ref, i, z, messages, i)
    for z in range(levels):
        above = [e0_ref[i, z + 1] for i in range(2)] if z + 1 < levels else [zero, zero]
        h_here = [read_wide(h_ref, i, z, messages, 3 + i) for i in range(3)]
        new = magnetic([e0_ref[i, z] for i in range(3)], above, h_here, zero_row, zero_row, keep)
        for i in range(3):
            h1_ref[i, z] = new[i]
    inv = []
    for z in range(levels):
        below = [h1_ref[i, z - 1] for i in range(2)] if z else [zero, zero]
        curl = curl_back([h1_ref[i, z] for i in range(3)], below, zero_row, zero_row)
        inv.append(read_wide(k_ref, 0, z, messages, 9))
        for i in range(3):
            e1_ref[i, z] = read_wide(d_ref, i, z, messages, 6 + i) + inv[z] * curl[i]
    even = lax.rem(lax.axis_index("gx"), 2) == 0
    keep_row = kept_lanes((1, wide[1]), width)
    end = slice(rows - 1, rows)
    for z in range(levels):
        hy, hz = h1_ref[1, z, end], h1_ref[2, z, end]
        ex, ey, ez = (e1_ref[i, z, end] for i in range(3))
        up_x = e1_ref[0, z + 1, end] if z + 1 < levels else zero_row
        second_y = hy - COURANT * ((up_x - ex) + ez)
        second_z = hz - COURANT * (-ey - (ahead_y(ex) - ex))
        up = [hy, hz, jnp.where(keep_row, second_y, 0.0), jnp.where(keep_row, second_z, 0.0), inv[z][end]]
        down = [e0_ref[1, z, 0:1], e0_ref[2, z, 0:1], e1_ref[1, z, 0:1], e1_ref[2, z, 0:1], inv[z][0:1]]
        for k in range(5):
            out_one_ref[k, z : z + 1] = jnp.where(even, up[k], down[k])
            out_two_ref[k, z : z + 1] = jnp.where(even, down[k], up[k])


def first_step(e_field, h_field, local, factors, one, two, tie):
    _, levels, rows, width = e_field.shape
    message = jax.ShapeDtypeStruct((5, levels, width + LANES), jnp.float32)
    store = (3, levels, rows, width + LANES)
    field = jax.ShapeDtypeStruct(store, jnp.float32)
    vmem = pl.BlockSpec(memory_space=pltpu.VMEM)
    return pl.pallas_call(
        first_body,
        out_shape=(message, message, field, field),
        in_specs=[vmem] * 6 + [pl.BlockSpec(memory_space=pl.ANY)],
        scratch_shapes=[pltpu.VMEM(store, jnp.float32)],
        compiler_params=VMEM,
        name="first_step",
    )(e_field, h_field, local, factors, one, two, tie)


def store_plane(plane_ref, surface_ref, number, layer, part, value):
    rows, half = value.shape[0], plane_ref.shape[2]
    at = ((number * 2 + layer) * 4 + part) * rows
    weighted = value[:, : 2 * half] * surface_ref[layer].astype(jnp.float32)
    plane_ref[0, at : at + rows] = weighted[:, :half]
    plane_ref[1, at : at + rows] = weighted[:, half:]


def split_planes(plane_ref, split_refs, rows, pairs):
    kinds = 16
    half = plane_ref.shape[2]
    count = split_refs[0].shape[0] // 2
    back = half - 1 - lane_index((kinds, half))
    for turn, v in enumerate(pairs):
        high = [plane_ref[side, pl.ds(rows // 2 + v, kinds, stride=rows), :] for side in range(2)]
        low = [plane_ref[side, pl.ds(rows // 2 - 1 - v, kinds, stride=rows), :] for side in range(2)]
        for parity in range(2):
            left, right = (b - a if parity else b + a for a, b in zip(low, high))
            left = jnp.take_along_axis(left, back, axis=1)
            at = slice((2 * turn + parity) * kinds, (2 * turn + parity + 1) * kinds)
            below = slice(count + at.start, count + at.stop)
            for value, ref in zip((right + left, right - left), split_refs):
                top = value.astype(jnp.bfloat16)
                ref[at, :half] = top
                ref[at, half:] = top
                ref[below, :half] = (value - top.astype(jnp.float32)).astype(jnp.bfloat16)
                ref[below, half:] = jnp.zeros_like(top)


def project_chunk(split_refs, cos_ref, sin_ref, phase_ref, cut, pairs):
    even_ref, odd_ref = split_refs
    count = even_ref.shape[0] // 2
    part_c = jnp.dot(even_ref[...], cos_ref[:, cut], preferred_element_type=jnp.float32)
    part_s = jnp.dot(odd_ref[...], sin_ref[:, cut], preferred_element_type=jnp.float32)
    part_c = part_c[:count] + part_c[count:]
    part_s = part_s[:count] + part_s[count:]
    real = [0.0, 0.0]
    imag = [0.0, 0.0]
    for turn, v in enumerate(pairs):
        cos_x = phase_ref[v : v + 1, cut]
        sin_x = phase_ref[8 + v : 9 + v, cut]
        for n in range(2):
            same = slice((turn * 4 + n) * 8, (turn * 4 + n) * 8 + 8)
            flip = slice((turn * 4 + 2 + n) * 8, (turn * 4 + 2 + n) * 8 + 8)
            real[n] = real[n] + (cos_x * part_c[same] - sin_x * part_s[flip])
            imag[n] = imag[n] + (cos_x * part_s[same] + sin_x * part_c[flip])
    sum_real = 0.0
    sum_imag = 0.0
    for n in range(2):
        cos_n, sin_n = math.cos(OMEGA * (n + 1)), math.sin(OMEGA * (n + 1))
        sum_real = sum_real + (cos_n * real[n] + sin_n * imag[n])
        sum_imag = sum_imag + (cos_n * imag[n] - sin_n * real[n])
    cos_c, sin_c = phase_ref[16:24, cut], phase_ref[24:32, cut]
    return sum_real * cos_c - sum_imag * sin_c, sum_real * sin_c + sum_imag * cos_c


def split_shapes(pairs, width):
    return [(2 * 32 * len(pairs), width)] * 2


def inside_body(h1_ref, e1_ref, g_ref, k_ref, surface_ref, cos_ref, sin_ref, phase_ref, out_ref, plane_ref, *split_refs, pairs):
    _, levels, rows, _ = h1_ref.shape
    width = g_ref.shape[3]
    wide = (rows, h1_ref.shape[3])
    keep = kept_lanes(wide, width)
    zero_row = jnp.zeros((1, wide[1]), jnp.float32)
    zero = jnp.zeros(wide, jnp.float32)

    def second(z):
        above = [e1_ref[i, z + 1] for i in range(2)] if z + 1 < levels else [zero, zero]
        here = [e1_ref[i, z] for i in range(3)]
        return magnetic(here, above, [h1_ref[i, z] for i in range(3)], zero_row, zero_row, keep)

    for layer, z in enumerate((0, levels - 1)):
        h2 = second(z)
        below = second(z - 1)[:2] if z else [zero, zero]
        curl = curl_back(h2, below, zero_row, zero_row)
        for i in range(2):
            store_plane(plane_ref, surface_ref, 0, layer, i, e1_ref[i, z])
            store_plane(plane_ref, surface_ref, 0, layer, 2 + i, h1_ref[i, z])
            new = k_ref[1, z] * e1_ref[i, z, :, :width] + k_ref[0, z] * curl[i][:, :width] - g_ref[i, z]
            store_plane(plane_ref, surface_ref, 1, layer, i, new)
            store_plane(plane_ref, surface_ref, 1, layer, 2 + i, h2[i])
    split_planes(plane_ref, split_refs, rows, pairs)
    chunk = 256
    for at in range(0, out_ref.shape[1], chunk):
        cut = slice(at, at + chunk)
        out_ref[0:8, cut], out_ref[8:16, cut] = project_chunk(split_refs, cos_ref, sin_ref, phase_ref, cut, pairs)


def inside(h1, e1, late, factors, surface, cos_y, sin_y, phases):
    _, _, rows, width = late.shape
    pairs = range(rows // 2 - 2)
    count = cos_y.shape[1]
    return pl.pallas_call(
        partial(inside_body, pairs=pairs),
        out_shape=jax.ShapeDtypeStruct((16, count), jnp.float32),
        scratch_shapes=[pltpu.VMEM((2, 16 * rows, width // 2), jnp.float32)]
        + [pltpu.VMEM(shape, jnp.bfloat16) for shape in split_shapes(pairs, width)],
        compiler_params=VMEM,
        cost_estimate=pl.CostEstimate(
            flops=8 * 32 * len(pairs) * width * count, bytes_accessed=4 * width * count, transcendentals=0
        ),
        name="inside",
    )(h1, e1, late, factors, surface, cos_y, sin_y, phases)


def second_body(h1_in, e1_in, g_ref, k_ref, surface_ref, own_one_ref, own_two_ref, x_one_ref, x_two_ref, e_out, h_out,
                even_ref, odd_ref, h1_ref, e1_ref, h2_ref, plane_ref, *, pairs):
    _, levels, rows, _ = h1_in.shape
    width = g_ref.shape[3]
    wide = (rows, h1_in.shape[3])
    keep = kept_lanes(wide, width)
    keep_row = kept_lanes((1, wide[1]), width)
    zero_row = jnp.zeros((1, wide[1]), jnp.float32)
    zero = jnp.zeros(wide, jnp.float32)
    at_row = row_index(wide)
    place, count = lax.axis_index("gx"), lax.axis_size("gx")
    even = lax.rem(place, 2) == 0
    has_before, has_after = place > 0, place < count - 1
    first, end = slice(0, 1), slice(rows - 1, rows)
    layers = {0: 0, levels - 1: 1}

    def from_before(k, z):
        got = jnp.where(even, x_two_ref[k, z : z + 1], x_one_ref[k, z : z + 1])
        return jnp.where(has_before, got, 0.0)

    def from_after(k, z):
        got = jnp.where(even, x_one_ref[k, z : z + 1], x_two_ref[k, z : z + 1])
        return jnp.where(has_after, got, 0.0)

    def own_up(k, z):
        return jnp.where(even, own_one_ref[k, z : z + 1], own_two_ref[k, z : z + 1])

    def own_down(k, z):
        return jnp.where(even, own_two_ref[k, z : z + 1], own_one_ref[k, z : z + 1])

    def patched(value, start, stop):
        if start is not None:
            value = jnp.where(at_row == 0, value + start, value)
        return jnp.where(at_row == rows - 1, value + stop, value)

    diff_y = [jnp.where(has_before, COURANT * own_down(1, z), 0.0) for z in range(levels)]
    diff_z = [jnp.where(has_before, -COURANT * own_down(0, z), 0.0) for z in range(levels)]
    last_y = [COURANT * from_after(1, z) for z in range(levels)]
    last_z = [-COURANT * from_after(0, z) for z in range(levels)]
    for z in range(levels):
        h1 = [h1_in[0, z], patched(h1_in[1, z], None, last_y[z]), patched(h1_in[2, z], None, last_z[z])]
        low = last_y[z - 1] if z else zero_row
        inv, inv_first = own_up(4, z), own_down(4, z)
        stop_x = inv * ((last_z[z] - behind_y(last_z[z])) - (last_y[z] - low))
        start_y = inv_first * (from_before(1, z) + diff_z[z])
        start_z = -inv_first * (from_before(0, z) + diff_y[z])
        e1 = [
            patched(e1_in[0, z], None, stop_x),
            patched(e1_in[1, z], start_y, -inv * last_z[z]),
            patched(e1_in[2, z], start_z, inv * last_y[z]),
        ]
        for i in range(3):
            h1_ref[i, z] = h1[i]
            e1_ref[i, z] = e1[i]
        if z in layers:
            for i in range(2):
                store_plane(plane_ref, surface_ref, 0, layers[z], i, e1[i])
                store_plane(plane_ref, surface_ref, 0, layers[z], 2 + i, h1[i])

    for z in range(levels):
        above = [e1_ref[i, z + 1] for i in range(2)] if z + 1 < levels else [zero, zero]
        inv = from_after(4, z)
        row_y = from_after(2, z) + inv * h1_ref[2, z, end]
        row_z = from_after(3, z) - inv * h1_ref[1, z, end]
        new = magnetic(
            [e1_ref[i, z] for i in range(3)], above, [h1_ref[i, z] for i in range(3)], row_y, row_z, keep
        )
        for i in range(3):
            h2_ref[i, z] = new[i]
            h_out[i, z] = new[i][:, :width]
        if z in layers:
            for i in range(2):
                store_plane(plane_ref, surface_ref, 1, layers[z], 2 + i, new[i])

    inv_before = [from_before(4, z) for z in range(levels)]
    diff_ex = []
    for z in range(levels):
        low = diff_y[z - 1] if z else zero_row
        diff_ex.append(inv_before[z] * ((diff_z[z] - behind_y(diff_z[z])) - (diff_y[z] - low)))
    for z in range(levels):
        below = [h2_ref[i, z - 1] for i in range(2)] if z else [zero, zero]
        up = diff_ex[z + 1] if z + 1 < levels else zero_row
        diff_ey = -inv_before[z] * diff_z[z]
        diff_ez = inv_before[z] * diff_y[z]
        row_y = from_before(2, z) + diff_y[z] - COURANT * ((up - diff_ex[z]) - (e1_ref[2, z, first] - diff_ez))
        row_z = from_before(3, z) + diff_z[z] - COURANT * (
            (e1_ref[1, z, first] - diff_ey) - (ahead_y(diff_ex[z]) - diff_ex[z])
        )
        open_row = keep_row & has_before
        row_y = jnp.where(open_row, row_y, 0.0)
        row_z = jnp.where(open_row, row_z, 0.0)
        curl = curl_back([h2_ref[i, z] for i in range(3)], below, row_y, row_z)
        for i in range(3):
            new = k_ref[1, z] * e1_ref[i, z, :, :width] + k_ref[0, z] * curl[i][:, :width] - g_ref[i, z]
            e_out[i, z] = new
            if i < 2 and z in layers:
                store_plane(plane_ref, surface_ref, 1, layers[z], i, new)
    split_planes(plane_ref, (even_ref, odd_ref), rows, pairs)


def edge_pairs(rows):
    return range(rows // 2 - 2, rows // 2)


def second_step(h1, e1, late, factors, surface, own_one, own_two, x_one, x_two):
    _, _, rows, width = late.shape
    pairs = edge_pairs(rows)
    field = jax.ShapeDtypeStruct(late.shape, jnp.float32)
    store = pltpu.VMEM(h1.shape, jnp.float32)
    return pl.pallas_call(
        partial(second_body, pairs=pairs),
        out_shape=(pltpu.VMEM(late.shape, jnp.float32), pltpu.VMEM(late.shape, jnp.float32))
        + tuple(jax.ShapeDtypeStruct(shape, jnp.bfloat16) for shape in split_shapes(pairs, width)),
        scratch_shapes=[store, store, store, pltpu.VMEM((2, 16 * rows, width // 2), jnp.float32)],
        compiler_params=VMEM,
        name="second_step",
    )(h1, e1, late, factors, surface, own_one, own_two, x_one, x_two)


def table_body(waves_ref, cos_ref, sin_ref, phase_ref, centre_ref, *, rows, width, scale, owned):
    half = width // 2
    chunk = TABLE_CHUNK
    chunks = waves_ref.shape[1] // chunk
    step = (row_index((8, chunk)).astype(jnp.float32)) + 0.5
    centre_x = (lax.axis_index("gx") * rows).astype(jnp.float32) + 0.5 * (rows - 1)
    centre_y = (lax.axis_index("gy") * width).astype(jnp.float32) + 0.5 * (width - 1)
    for k in range(chunks):
        cut = slice(k * chunk, (k + 1) * chunk)
        centre_ref[0, k : k + 1] = WAVE * waves_ref[0:1, cut] * centre_x + WAVE * waves_ref[1:2, cut] * centre_y
    sin_c, cos_c = sincos(centre_ref[0])
    centre_ref[0] = scale * cos_c
    centre_ref[1] = scale * sin_c

    @pl.loop(0, chunks, unroll=2)
    def _(turn):
        cut = pl.ds(pl.multiple_of(turn * chunk, chunk), chunk)
        source = block_source(turn, owned // chunk) if owned % chunk == 0 else turn
        at = pl.ds(pl.multiple_of(source * chunk, chunk), chunk)
        wave_x, wave_y = WAVE * waves_ref[0:1, at], WAVE * waves_ref[1:2, at]
        sin_x, cos_x = sincos(wave_x * step)
        phase_ref[0:8, cut] = cos_x
        phase_ref[8:16, cut] = sin_x
        phase_ref[16:24, cut] = jnp.broadcast_to(centre_ref[0, pl.ds(source, 1)], step.shape)
        phase_ref[24:32, cut] = jnp.broadcast_to(centre_ref[1, pl.ds(source, 1)], step.shape)
        sin_y, cos_y = sincos(wave_y * step)
        cos_w = cos_y[7:8] * cos_y[0:1] - sin_y[7:8] * sin_y[0:1]
        sin_w = sin_y[7:8] * cos_y[0:1] + cos_y[7:8] * sin_y[0:1]
        next_cos = cos_y * cos_w - sin_y * sin_w
        next_sin = sin_y * cos_w + cos_y * sin_w
        cos_y = jnp.concatenate([cos_y, next_cos], axis=0)
        sin_y = jnp.concatenate([sin_y, next_sin], axis=0)
        sin_w, cos_w = 2.0 * sin_w * cos_w, 1.0 - 2.0 * sin_w * sin_w
        for start in range(0, half, 16):
            if start:
                cos_y, sin_y = cos_y * cos_w - sin_y * sin_w, sin_y * cos_w + cos_y * sin_w
            for value, ref in ((cos_y, cos_ref), (sin_y, sin_ref)):
                top = value.astype(jnp.bfloat16)
                ref[start : start + 16, cut] = top
                ref[half + start : half + start + 16, cut] = (value - top.astype(jnp.float32)).astype(jnp.bfloat16)


def block_source(block, each):
    count_x, count_y = lax.axis_size("gx"), lax.axis_size("gy")
    group = group_of("gx")
    place_x, place_y = lax.axis_index("gx"), lax.axis_index("gy")
    rest, within = block // each, block % each
    rest, far_y = rest // (count_y // 2), rest % (count_y // 2)
    rest, near_x = rest // group, rest % group
    core, far_x = rest // (count_x // group), rest % (count_x // group)
    owner_x = (far_x ^ (place_x // group)) * group + (place_x + near_x) % group
    owner_y = (far_y ^ (place_y // 2)) * 2 + (core ^ (place_y % 2))
    return (owner_x * count_y + owner_y) * each + within


def tables(waves, rows, width, scale):
    count = waves.shape[1]
    owned = count // (lax.axis_size("gx") * lax.axis_size("gy"))
    table = jax.ShapeDtypeStruct((width, count), jnp.bfloat16)
    return pl.pallas_call(
        partial(table_body, rows=rows, width=width, scale=scale, owned=owned),
        out_shape=(table, table, jax.ShapeDtypeStruct((32, count), jnp.float32)),
        scratch_shapes=[pltpu.VMEM((2, count // TABLE_CHUNK, TABLE_CHUNK), jnp.float32)],
        compiler_params=VMEM,
        cost_estimate=pl.CostEstimate(flops=40 * width * count, bytes_accessed=4 * width * count, transcendentals=0),
        name="tables",
    )(waves)


def project_body(even_ref, odd_ref, cos_ref, sin_ref, phase_ref, inner_ref, out_ref, *, start, pairs):
    chunk = 256
    for at in range(0, out_ref.shape[1], chunk):
        cut, to = slice(start + at, start + at + chunk), slice(at, at + chunk)
        real, imag = project_chunk((even_ref, odd_ref), cos_ref, sin_ref, phase_ref, cut, pairs)
        out_ref[0:8, to] = real + inner_ref[0:8, cut]
        out_ref[8:16, to] = imag + inner_ref[8:16, cut]


def project(planes, cos_y, sin_y, phases, inner, rows, start, count):
    width = cos_y.shape[0]
    return pl.pallas_call(
        partial(project_body, start=start, pairs=edge_pairs(rows)),
        out_shape=jax.ShapeDtypeStruct((16, count), jnp.float32),
        compiler_params=VMEM,
        cost_estimate=pl.CostEstimate(
            flops=8 * planes[0].shape[0] * width * count, bytes_accessed=4 * width * count, transcendentals=0
        ),
        name="project",
    )(*planes, cos_y, sin_y, phases, inner)


def swap(array, axis, mask):
    return lax.ppermute(array, axis, [(i, i ^ mask) for i in range(lax.axis_size(axis))])


def swap_other(array, axis):
    pairs = [(i, ((i + 1) ^ 1) - 1) for i in range(1, lax.axis_size(axis) - 1)]
    return lax.ppermute(array, axis, pairs)


def group_of(axis):
    return min(lax.axis_size(axis), 4)


def own_first(directions):
    count_x, count_y = lax.axis_size("gx"), lax.axis_size("gy")
    group = group_of("gx")
    waves = directions.T.reshape(2, count_x // group, group, count_y // 2, 2, -1)
    place_x, place_y = lax.axis_index("gx"), lax.axis_index("gy")
    waves = jnp.where(place_y % 2 == 1, jnp.flip(waves, 4), waves)
    waves = lax.dynamic_slice_in_dim(jnp.concatenate([waves, waves], axis=2), place_x % group, group, axis=2)
    waves = exclusive(waves, 1, place_x // group)
    waves = exclusive(waves, 3, place_y // 2)
    return waves.transpose(0, 4, 1, 2, 3, 5).reshape(2, directions.shape[0])


def exclusive(array, axis, place):
    size = array.shape[axis]
    bit = 1
    while bit < size:
        pieces = jnp.split(array, size // bit, axis)
        turned = jnp.concatenate([pieces[i ^ 1] for i in range(len(pieces))], axis)
        array = jnp.where(place & bit, turned, array)
        bit = 2 * bit
    return array


def halve(far, axis, mask):
    half = far.shape[1] // 2
    return far[:, :half] + swap(far[:, half:], axis, mask)


def halve_all(far, axis, low, size):
    mask = size // 2
    while mask >= 1:
        far = halve(far, axis, mask * low)
        mask = mask // 2
    return far


def scatter_group(far, axis):
    count, group = lax.axis_size(axis), group_of(axis)
    part = far.shape[1] // group
    total = far[:, :part]
    got = []
    for step in sorted(range(1, group), key=lambda step: (step != group // 2, step)):
        pairs = [(i, i // group * group + (i + step) % group) for i in range(count)]
        got.append(lax.ppermute(far[:, step * part : (step + 1) * part], axis, pairs))
    for array in got:
        total = total + array
    return total


def local(e_field, h_field, pol_now, pol_old, eps_inf, materials, surface, poles, directions):
    _, _, rows, width = e_field.shape
    scale = 1.0 / math.sqrt(rows * lax.axis_size("gx") * width * lax.axis_size("gy"))
    owned = directions.shape[0] // (lax.axis_size("gx") * lax.axis_size("gy"))
    waves = directions.T if owned % TABLE_CHUNK == 0 else own_first(directions)
    message, near, late, factors, e_field, h_field, waves = prepare(
        e_field, h_field, pol_now, pol_old, eps_inf, materials, poles, waves
    )
    one = swap(message, "gy", 1)
    two = swap_other(message, "gy")
    cos_y, sin_y, phases = tables(waves, rows, width, scale)
    own_one, own_two, h1, e1 = first_step(e_field, h_field, near, factors, one, two, phases)
    x_one = swap(own_one, "gx", 1)
    x_two = swap_other(own_two, "gx")
    inner = inside(h1, e1, late, factors, surface, cos_y, sin_y, phases)
    e_new, h_new, *planes = second_step(h1, e1, late, factors, surface, own_one, own_two, x_one, x_two)
    half = directions.shape[0] // 2
    far = project(planes, cos_y, sin_y, phases, inner, rows, half, half)
    arrived = swap(far, "gy", 1)
    far = project(planes, cos_y, sin_y, phases, inner, rows, 0, half) + arrived
    far = halve_all(far, "gx", group_of("gx"), lax.axis_size("gx") // group_of("gx"))
    far = scatter_group(far, "gx")
    far = halve_all(far, "gy", 2, lax.axis_size("gy") // 2)
    return e_new, h_new, far.T


def solution(mesh):
    field = P("design", None, "gx", "gy")
    cell = P("design", "gx", "gy")
    return jax.shard_map(
        local,
        mesh=mesh,
        in_specs=(field, field, field, field, cell, cell, cell, P(), P()),
        out_specs=(field, field, P(("gx", "gy"), "design")),
        check_vma=False,
    )
```

```python
from functools import partial
import math

import jax
import jax.numpy as jnp
from jax import lax
from jax.experimental import pallas as pl
from jax.experimental.pallas import tpu as pltpu
from jax.sharding import PartitionSpec as P

COURANT = 0.5
WAVE = 0.3
OMEGA = 0.25
LANES = 128
GROUPS = 2
TABLE_CHUNK = 256
SLOT = 40
PACKED = LANES // SLOT
VMEM = pltpu.CompilerParams(vmem_limit_bytes=24 * 1024 * 1024)


def lane_index(shape):
    return lax.broadcasted_iota(jnp.int32, shape, len(shape) - 1)


def row_index(shape):
    return lax.broadcasted_iota(jnp.int32, shape, 0)


def sincos(angle):
    turns = jnp.round(angle * (0.5 / math.pi))
    rest = angle - turns * 6.28125
    rest = rest - turns * 0.0019350051879882812
    rest = rest - turns * 3.0199159819567e-07
    half = 0.5 * rest
    sq = half * half
    sin_half = 1.0 / 6227020800.0
    for term in (-1.0 / 39916800.0, 1.0 / 362880.0, -1.0 / 5040.0, 1.0 / 120.0, -1.0 / 6.0, 1.0):
        sin_half = sin_half * sq + term
    sin_half = sin_half * half
    cos_half = -1.0 / 87178291200.0
    for term in (1.0 / 479001600.0, -1.0 / 3628800.0, 1.0 / 40320.0, -1.0 / 720.0, 1.0 / 24.0, -0.5, 1.0):
        cos_half = cos_half * sq + term
    return 2.0 * sin_half * cos_half, 1.0 - 2.0 * sin_half * sin_half


def prepare_body(e_in, h_in, p_in, q_in, eps_in, mat_in, poles_in, waves_in, message_ref, d_ref, g_ref, k_ref,
                 e_ref, h_ref, waves_ref, p_ref, q_ref, eps_ref, mat_ref, poles_ref, table_ref, sems, small_sems):
    levels, rows, width = eps_ref.shape
    last = width - LANES
    pairs = ((e_in, e_ref), (h_in, h_ref), (p_in, p_ref), (q_in, q_ref), (eps_in, eps_ref), (mat_in, mat_ref))
    poles_copy = pltpu.make_async_copy(poles_in, poles_ref, small_sems.at[0])
    poles_copy.start()
    copies = []
    cuts = (0, PACKED, levels)
    for part in range(GROUPS):
        cut = pl.ds(cuts[part], cuts[part + 1] - cuts[part])
        for k, (source, target) in enumerate(pairs):
            at = (slice(None), cut) if len(source.shape) == 4 else (cut,)
            copy = pltpu.make_async_copy(source.at[at], target.at[at], sems.at[part, k])
            copy.start()
            copies.append(copy)
    waves_copy = pltpu.make_async_copy(waves_in, waves_ref, small_sems.at[1])
    waves_copy.start()
    poles_copy.wait()
    table_ref[0:3, 0 : poles_ref.shape[1]] = poles_ref[...]
    omega_dt, gamma_dt, strength = (table_ref[i : i + 1, :] for i in range(3))
    denominator = 1.0 + 0.5 * gamma_dt
    tile = (rows, LANES)
    table_a = jnp.broadcast_to((2.0 - omega_dt * omega_dt) / denominator, tile)
    table_b = jnp.broadcast_to(-(1.0 - 0.5 * gamma_dt) / denominator, tile)
    table_c = jnp.broadcast_to(strength * omega_dt * omega_dt / denominator, tile)
    lane = lane_index(tile)
    for z in range(levels):
        if z in cuts:
            for copy in copies[cuts.index(z) * 6 : cuts.index(z) * 6 + 6]:
                copy.wait()
        if z % PACKED == 0:
            message = jnp.zeros(tile, jnp.float32)
        base = z % PACKED * SLOT
        edges = []
        for start in range(0, width, LANES):
            cut = slice(start, start + LANES)
            number = mat_ref[z, :, cut]
            a = jnp.take_along_axis(table_a, number, axis=1)
            b = jnp.take_along_axis(table_b, number, axis=1)
            c = jnp.take_along_axis(table_c, number, axis=1)
            inv = 1.0 / eps_ref[z, :, cut]
            half = COURANT * inv
            k_ref[0, z, :, cut] = half
            k_ref[1, z, :, cut] = 1.0 - c * inv
            items = [e_ref[i, z, :, cut] for i in range(3)] + [h_ref[i, z, :, cut] for i in range(3)]
            for i in range(3):
                now, old = p_ref[i, z, :, cut], q_ref[i, z, :, cut]
                new = a * now + b * old + c * items[i]
                local = items[i] - (new - now) * inv
                d_ref[i, z, :, cut] = local
                g_ref[i, z, :, cut] = ((a * new - new) + b * now) * inv
                items.append(local)
            items.append(half)
            if start in (0, last):
                edges.append(items)
        for k, (left, right) in enumerate(zip(edges[0], edges[-1])):
            at = base + 4 * k
            item = pltpu.roll(jnp.where(lane < 2, left, right), at + 2, 1)
            message = jnp.where((lane >= at) & (lane < at + 4), item, message)
        if z % PACKED == PACKED - 1 or z == levels - 1:
            message_ref[z // PACKED] = message
    waves_copy.wait()


def prepare(e_field, h_field, pol_now, pol_old, eps_inf, materials, poles, waves):
    levels, rows, width = eps_inf.shape
    message = jax.ShapeDtypeStruct((-(-levels // PACKED), rows, LANES), jnp.float32)
    field = jax.ShapeDtypeStruct(e_field.shape, jnp.float32)
    pair = jax.ShapeDtypeStruct((2, levels, rows, width), jnp.float32)
    arrays = (e_field, h_field, pol_now, pol_old, eps_inf, materials, poles, waves)
    return pl.pallas_call(
        prepare_body,
        out_shape=(message, field, field, pair, field, field, jax.ShapeDtypeStruct(waves.shape, jnp.float32)),
        in_specs=[pl.BlockSpec(memory_space=pltpu.HBM)] * 8,
        scratch_shapes=[
            pltpu.VMEM(e_field.shape, jnp.float32),
            pltpu.VMEM(e_field.shape, jnp.float32),
            pltpu.VMEM(eps_inf.shape, jnp.float32),
            pltpu.VMEM(eps_inf.shape, jnp.int32),
            pltpu.VMEM(poles.shape, jnp.float32),
            pltpu.VMEM((8, LANES), jnp.float32),
            pltpu.SemaphoreType.DMA((GROUPS, 6)),
            pltpu.SemaphoreType.DMA((2,)),
        ],
        compiler_params=VMEM,
        name="prepare",
    )(*(pltpu.with_memory_space_constraint(array, pltpu.HBM) for array in arrays))


def read_wide(own_ref, index, z, messages, item):
    both = messages[z // PACKED]
    lane = lane_index(both.shape)
    both = pltpu.roll(both, LANES - 2 - (z % PACKED * SLOT + 4 * item), 1)
    halo = jnp.where((lane < 2) | (lane >= LANES - 2), both, 0.0)
    return jnp.concatenate([own_ref[index, z], halo], axis=1)


def read_y_messages(one_ref, two_ref):
    place = lax.axis_index("gy")
    even = lax.rem(place, 2) == 0
    messages = []
    for k in range(one_ref.shape[0]):
        one, two = one_ref[k], two_ref[k]
        before = jnp.where(place > 0, jnp.where(even, two, one), 0.0)
        after = jnp.where(place < lax.axis_size("gy") - 1, jnp.where(even, one, two), 0.0)
        messages.append(jnp.where(lane_index(one.shape) % 4 < 2, before, after))
    return messages


def ahead_y(v):
    return pltpu.roll(v, v.shape[1] - 1, 1)


def behind_y(v):
    return pltpu.roll(v, 1, 1)


def ahead_x(v, row):
    at = row_index(v.shape)
    return jnp.where(at == v.shape[0] - 1, row, pltpu.roll(v, v.shape[0] - 1, 0))


def behind_x(v, row):
    at = row_index(v.shape)
    return jnp.where(at == 0, row, pltpu.roll(v, 1, 0))


def magnetic(e_here, e_above, h_here, row_y, row_z, keep):
    ex, ey, ez = e_here
    hx, hy, hz = h_here
    up_x, up_y = e_above
    hx = hx - COURANT * ((ahead_y(ez) - ez) - (up_y - ey))
    hy = hy - COURANT * ((up_x - ex) - (ahead_x(ez, row_z) - ez))
    hz = hz - COURANT * ((ahead_x(ey, row_y) - ey) - (ahead_y(ex) - ex))
    return [jnp.where(keep, v, 0.0) for v in (hx, hy, hz)]


def curl_back(h_here, h_below, row_y, row_z):
    hx, hy, hz = h_here
    low_x, low_y = h_below
    return (
        (hz - behind_y(hz)) - (hy - low_y),
        (hx - low_x) - (hz - behind_x(hz, row_z)),
        (hy - behind_x(hy, row_y)) - (hx - behind_y(hx)),
    )


def kept_lanes(shape, width):
    return (lane_index(shape) < width + LANES // 2) | (lax.axis_index("gy") > 0)


def first_body(e_ref, h_ref, d_ref, k_ref, one_ref, two_ref, tie_ref, out_one_ref, out_two_ref, h1_ref, e1_ref, e0_ref):
    del tie_ref
    _, levels, rows, width = e_ref.shape
    wide = (rows, width + LANES)
    messages = read_y_messages(one_ref, two_ref)
    keep = kept_lanes(wide, width)
    zero_row = jnp.zeros((1, wide[1]), jnp.float32)
    zero = jnp.zeros(wide, jnp.float32)
    for z in range(levels):
        for i in range(3):
            e0_ref[i, z] = read_wide(e_ref, i, z, messages, i)
    for z in range(levels):
        above = [e0_ref[i, z + 1] for i in range(2)] if z + 1 < levels else [zero, zero]
        h_here = [read_wide(h_ref, i, z, messages, 3 + i) for i in range(3)]
        new = magnetic([e0_ref[i, z] for i in range(3)], above, h_here, zero_row, zero_row, keep)
        for i in range(3):
            h1_ref[i, z] = new[i]
    inv = []
    for z in range(levels):
        below = [h1_ref[i, z - 1] for i in range(2)] if z else [zero, zero]
        curl = curl_back([h1_ref[i, z] for i in range(3)], below, zero_row, zero_row)
        inv.append(read_wide(k_ref, 0, z, messages, 9))
        for i in range(3):
            e1_ref[i, z] = read_wide(d_ref, i, z, messages, 6 + i) + inv[z] * curl[i]
    even = lax.rem(lax.axis_index("gx"), 2) == 0
    keep_row = kept_lanes((1, wide[1]), width)
    end = slice(rows - 1, rows)
    for z in range(levels):
        hy, hz = h1_ref[1, z, end], h1_ref[2, z, end]
        ex, ey, ez = (e1_ref[i, z, end] for i in range(3))
        up_x = e1_ref[0, z + 1, end] if z + 1 < levels else zero_row
        second_y = hy - COURANT * ((up_x - ex) + ez)
        second_z = hz - COURANT * (-ey - (ahead_y(ex) - ex))
        up = [hy, hz, jnp.where(keep_row, second_y, 0.0), jnp.where(keep_row, second_z, 0.0), inv[z][end]]
        down = [e0_ref[1, z, 0:1], e0_ref[2, z, 0:1], e1_ref[1, z, 0:1], e1_ref[2, z, 0:1], inv[z][0:1]]
        for k in range(5):
            out_one_ref[k, z : z + 1] = jnp.where(even, up[k], down[k])
            out_two_ref[k, z : z + 1] = jnp.where(even, down[k], up[k])


def first_step(e_field, h_field, local, factors, one, two, tie):
    _, levels, rows, width = e_field.shape
    message = jax.ShapeDtypeStruct((5, levels, width + LANES), jnp.float32)
    store = (3, levels, rows, width + LANES)
    field = jax.ShapeDtypeStruct(store, jnp.float32)
    vmem = pl.BlockSpec(memory_space=pltpu.VMEM)
    return pl.pallas_call(
        first_body,
        out_shape=(message, message, field, field),
        in_specs=[vmem] * 6 + [pl.BlockSpec(memory_space=pl.ANY)],
        scratch_shapes=[pltpu.VMEM(store, jnp.float32)],
        compiler_params=VMEM,
        name="first_step",
    )(e_field, h_field, local, factors, one, two, tie)


def store_plane(plane_ref, surface_ref, number, layer, part, value):
    rows, half = value.shape[0], plane_ref.shape[2]
    at = ((number * 2 + layer) * 4 + part) * rows
    weighted = value[:, : 2 * half] * surface_ref[layer].astype(jnp.float32)
    plane_ref[0, at : at + rows] = weighted[:, :half]
    plane_ref[1, at : at + rows] = weighted[:, half:]


def split_planes(plane_ref, split_refs, rows, pairs):
    kinds = 16
    half = plane_ref.shape[2]
    count = split_refs[0].shape[0] // 2
    back = half - 1 - lane_index((kinds, half))
    for turn, v in enumerate(pairs):
        high = [plane_ref[side, pl.ds(rows // 2 + v, kinds, stride=rows), :] for side in range(2)]
        low = [plane_ref[side, pl.ds(rows // 2 - 1 - v, kinds, stride=rows), :] for side in range(2)]
        for parity in range(2):
            left, right = (b - a if parity else b + a for a, b in zip(low, high))
            left = jnp.take_along_axis(left, back, axis=1)
            at = slice((2 * turn + parity) * kinds, (2 * turn + parity + 1) * kinds)
            below = slice(count + at.start, count + at.stop)
            for value, ref in zip((right + left, right - left), split_refs):
                top = value.astype(jnp.bfloat16)
                ref[at, :half] = top
                ref[at, half:] = top
                ref[below, :half] = (value - top.astype(jnp.float32)).astype(jnp.bfloat16)
                ref[below, half:] = jnp.zeros_like(top)


def project_chunk(split_refs, cos_ref, sin_ref, phase_ref, cut, pairs):
    even_ref, odd_ref = split_refs
    count = even_ref.shape[0] // 2
    part_c = jnp.dot(even_ref[...], cos_ref[:, cut], preferred_element_type=jnp.float32)
    part_s = jnp.dot(odd_ref[...], sin_ref[:, cut], preferred_element_type=jnp.float32)
    part_c = part_c[:count] + part_c[count:]
    part_s = part_s[:count] + part_s[count:]
    real = [0.0, 0.0]
    imag = [0.0, 0.0]
    for turn, v in enumerate(pairs):
        cos_x = phase_ref[v : v + 1, cut]
        sin_x = phase_ref[8 + v : 9 + v, cut]
        for n in range(2):
            same = slice((turn * 4 + n) * 8, (turn * 4 + n) * 8 + 8)
            flip = slice((turn * 4 + 2 + n) * 8, (turn * 4 + 2 + n) * 8 + 8)
            real[n] = real[n] + (cos_x * part_c[same] - sin_x * part_s[flip])
            imag[n] = imag[n] + (cos_x * part_s[same] + sin_x * part_c[flip])
    sum_real = 0.0
    sum_imag = 0.0
    for n in range(2):
        cos_n, sin_n = math.cos(OMEGA * (n + 1)), math.sin(OMEGA * (n + 1))
        sum_real = sum_real + (cos_n * real[n] + sin_n * imag[n])
        sum_imag = sum_imag + (cos_n * imag[n] - sin_n * real[n])
    cos_c, sin_c = phase_ref[16:24, cut], phase_ref[24:32, cut]
    return sum_real * cos_c - sum_imag * sin_c, sum_real * sin_c + sum_imag * cos_c


def split_shapes(pairs, width):
    return [(2 * 32 * len(pairs), width)] * 2


def inside_body(h1_ref, e1_ref, g_ref, k_ref, surface_ref, cos_ref, sin_ref, phase_ref, out_ref, plane_ref, *split_refs, pairs):
    _, levels, rows, _ = h1_ref.shape
    width = g_ref.shape[3]
    wide = (rows, h1_ref.shape[3])
    keep = kept_lanes(wide, width)
    zero_row = jnp.zeros((1, wide[1]), jnp.float32)
    zero = jnp.zeros(wide, jnp.float32)

    def second(z):
        above = [e1_ref[i, z + 1] for i in range(2)] if z + 1 < levels else [zero, zero]
        here = [e1_ref[i, z] for i in range(3)]
        return magnetic(here, above, [h1_ref[i, z] for i in range(3)], zero_row, zero_row, keep)

    for layer, z in enumerate((0, levels - 1)):
        h2 = second(z)
        below = second(z - 1)[:2] if z else [zero, zero]
        curl = curl_back(h2, below, zero_row, zero_row)
        for i in range(2):
            store_plane(plane_ref, surface_ref, 0, layer, i, e1_ref[i, z])
            store_plane(plane_ref, surface_ref, 0, layer, 2 + i, h1_ref[i, z])
            new = k_ref[1, z] * e1_ref[i, z, :, :width] + k_ref[0, z] * curl[i][:, :width] - g_ref[i, z]
            store_plane(plane_ref, surface_ref, 1, layer, i, new)
            store_plane(plane_ref, surface_ref, 1, layer, 2 + i, h2[i])
    split_planes(plane_ref, split_refs, rows, pairs)
    chunk = 512
    for at in range(0, out_ref.shape[1], chunk):
        cut = slice(at, at + chunk)
        out_ref[0:8, cut], out_ref[8:16, cut] = project_chunk(split_refs, cos_ref, sin_ref, phase_ref, cut, pairs)


def inside(h1, e1, late, factors, surface, cos_y, sin_y, phases):
    _, _, rows, width = late.shape
    pairs = range(rows // 2 - 2)
    count = cos_y.shape[1]
    return pl.pallas_call(
        partial(inside_body, pairs=pairs),
        out_shape=jax.ShapeDtypeStruct((16, count), jnp.float32),
        scratch_shapes=[pltpu.VMEM((2, 16 * rows, width // 2), jnp.float32)]
        + [pltpu.VMEM(shape, jnp.bfloat16) for shape in split_shapes(pairs, width)],
        compiler_params=VMEM,
        cost_estimate=pl.CostEstimate(
            flops=8 * 32 * len(pairs) * width * count, bytes_accessed=4 * width * count, transcendentals=0
        ),
        name="inside",
    )(h1, e1, late, factors, surface, cos_y, sin_y, phases)


def second_body(h1_in, e1_in, g_ref, k_ref, surface_ref, own_one_ref, own_two_ref, x_one_ref, x_two_ref, e_out, h_out,
                even_ref, odd_ref, h1_ref, e1_ref, h2_ref, plane_ref, *, pairs):
    _, levels, rows, _ = h1_in.shape
    width = g_ref.shape[3]
    wide = (rows, h1_in.shape[3])
    keep = kept_lanes(wide, width)
    keep_row = kept_lanes((1, wide[1]), width)
    zero_row = jnp.zeros((1, wide[1]), jnp.float32)
    zero = jnp.zeros(wide, jnp.float32)
    at_row = row_index(wide)
    place, count = lax.axis_index("gx"), lax.axis_size("gx")
    even = lax.rem(place, 2) == 0
    has_before, has_after = place > 0, place < count - 1
    first, end = slice(0, 1), slice(rows - 1, rows)
    layers = {0: 0, levels - 1: 1}

    def from_before(k, z):
        got = jnp.where(even, x_two_ref[k, z : z + 1], x_one_ref[k, z : z + 1])
        return jnp.where(has_before, got, 0.0)

    def from_after(k, z):
        got = jnp.where(even, x_one_ref[k, z : z + 1], x_two_ref[k, z : z + 1])
        return jnp.where(has_after, got, 0.0)

    def own_up(k, z):
        return jnp.where(even, own_one_ref[k, z : z + 1], own_two_ref[k, z : z + 1])

    def own_down(k, z):
        return jnp.where(even, own_two_ref[k, z : z + 1], own_one_ref[k, z : z + 1])

    def patched(value, start, stop):
        if start is not None:
            value = jnp.where(at_row == 0, value + start, value)
        return jnp.where(at_row == rows - 1, value + stop, value)

    diff_y = [jnp.where(has_before, COURANT * own_down(1, z), 0.0) for z in range(levels)]
    diff_z = [jnp.where(has_before, -COURANT * own_down(0, z), 0.0) for z in range(levels)]
    last_y = [COURANT * from_after(1, z) for z in range(levels)]
    last_z = [-COURANT * from_after(0, z) for z in range(levels)]
    for z in range(levels):
        h1 = [h1_in[0, z], patched(h1_in[1, z], None, last_y[z]), patched(h1_in[2, z], None, last_z[z])]
        low = last_y[z - 1] if z else zero_row
        inv, inv_first = own_up(4, z), own_down(4, z)
        stop_x = inv * ((last_z[z] - behind_y(last_z[z])) - (last_y[z] - low))
        start_y = inv_first * (from_before(1, z) + diff_z[z])
        start_z = -inv_first * (from_before(0, z) + diff_y[z])
        e1 = [
            patched(e1_in[0, z], None, stop_x),
            patched(e1_in[1, z], start_y, -inv * last_z[z]),
            patched(e1_in[2, z], start_z, inv * last_y[z]),
        ]
        for i in range(3):
            h1_ref[i, z] = h1[i]
            e1_ref[i, z] = e1[i]
        if z in layers:
            for i in range(2):
                store_plane(plane_ref, surface_ref, 0, layers[z], i, e1[i])
                store_plane(plane_ref, surface_ref, 0, layers[z], 2 + i, h1[i])

    for z in range(levels):
        above = [e1_ref[i, z + 1] for i in range(2)] if z + 1 < levels else [zero, zero]
        inv = from_after(4, z)
        row_y = from_after(2, z) + inv * h1_ref[2, z, end]
        row_z = from_after(3, z) - inv * h1_ref[1, z, end]
        new = magnetic(
            [e1_ref[i, z] for i in range(3)], above, [h1_ref[i, z] for i in range(3)], row_y, row_z, keep
        )
        for i in range(3):
            h2_ref[i, z] = new[i]
            h_out[i, z] = new[i][:, :width]
        if z in layers:
            for i in range(2):
                store_plane(plane_ref, surface_ref, 1, layers[z], 2 + i, new[i])

    inv_before = [from_before(4, z) for z in range(levels)]
    diff_ex = []
    for z in range(levels):
        low = diff_y[z - 1] if z else zero_row
        diff_ex.append(inv_before[z] * ((diff_z[z] - behind_y(diff_z[z])) - (diff_y[z] - low)))
    for z in range(levels):
        below = [h2_ref[i, z - 1] for i in range(2)] if z else [zero, zero]
        up = diff_ex[z + 1] if z + 1 < levels else zero_row
        diff_ey = -inv_before[z] * diff_z[z]
        diff_ez = inv_before[z] * diff_y[z]
        row_y = from_before(2, z) + diff_y[z] - COURANT * ((up - diff_ex[z]) - (e1_ref[2, z, first] - diff_ez))
        row_z = from_before(3, z) + diff_z[z] - COURANT * (
            (e1_ref[1, z, first] - diff_ey) - (ahead_y(diff_ex[z]) - diff_ex[z])
        )
        open_row = keep_row & has_before
        row_y = jnp.where(open_row, row_y, 0.0)
        row_z = jnp.where(open_row, row_z, 0.0)
        curl = curl_back([h2_ref[i, z] for i in range(3)], below, row_y, row_z)
        for i in range(3):
            new = k_ref[1, z] * e1_ref[i, z, :, :width] + k_ref[0, z] * curl[i][:, :width] - g_ref[i, z]
            e_out[i, z] = new
            if i < 2 and z in layers:
                store_plane(plane_ref, surface_ref, 1, layers[z], i, new)
    split_planes(plane_ref, (even_ref, odd_ref), rows, pairs)


def edge_pairs(rows):
    return range(rows // 2 - 2, rows // 2)


def second_step(h1, e1, late, factors, surface, own_one, own_two, x_one, x_two):
    _, _, rows, width = late.shape
    pairs = edge_pairs(rows)
    field = jax.ShapeDtypeStruct(late.shape, jnp.float32)
    store = pltpu.VMEM(h1.shape, jnp.float32)
    return pl.pallas_call(
        partial(second_body, pairs=pairs),
        out_shape=(pltpu.VMEM(late.shape, jnp.float32), pltpu.VMEM(late.shape, jnp.float32))
        + tuple(jax.ShapeDtypeStruct(shape, jnp.bfloat16) for shape in split_shapes(pairs, width)),
        scratch_shapes=[store, store, store, pltpu.VMEM((2, 16 * rows, width // 2), jnp.float32)],
        compiler_params=VMEM,
        name="second_step",
    )(h1, e1, late, factors, surface, own_one, own_two, x_one, x_two)


def table_body(waves_ref, cos_ref, sin_ref, phase_ref, centre_ref, *, rows, width, scale, owned):
    half = width // 2
    chunk = TABLE_CHUNK
    chunks = waves_ref.shape[1] // chunk
    step = (row_index((8, chunk)).astype(jnp.float32)) + 0.5
    centre_x = (lax.axis_index("gx") * rows).astype(jnp.float32) + 0.5 * (rows - 1)
    centre_y = (lax.axis_index("gy") * width).astype(jnp.float32) + 0.5 * (width - 1)
    for k in range(chunks):
        cut = slice(k * chunk, (k + 1) * chunk)
        centre_ref[0, k : k + 1] = WAVE * waves_ref[0:1, cut] * centre_x + WAVE * waves_ref[1:2, cut] * centre_y
    sin_c, cos_c = sincos(centre_ref[0])
    centre_ref[0] = scale * cos_c
    centre_ref[1] = scale * sin_c

    @pl.loop(0, chunks, unroll=2)
    def _(turn):
        cut = pl.ds(pl.multiple_of(turn * chunk, chunk), chunk)
        source = block_source(turn, owned // chunk) if owned % chunk == 0 else turn
        at = pl.ds(pl.multiple_of(source * chunk, chunk), chunk)
        wave_x, wave_y = WAVE * waves_ref[0:1, at], WAVE * waves_ref[1:2, at]
        sin_x, cos_x = sincos(wave_x * step)
        phase_ref[0:8, cut] = cos_x
        phase_ref[8:16, cut] = sin_x
        phase_ref[16:24, cut] = jnp.broadcast_to(centre_ref[0, pl.ds(source, 1)], step.shape)
        phase_ref[24:32, cut] = jnp.broadcast_to(centre_ref[1, pl.ds(source, 1)], step.shape)
        sin_y, cos_y = sincos(wave_y * step)
        cos_w = cos_y[7:8] * cos_y[0:1] - sin_y[7:8] * sin_y[0:1]
        sin_w = sin_y[7:8] * cos_y[0:1] + cos_y[7:8] * sin_y[0:1]
        next_cos = cos_y * cos_w - sin_y * sin_w
        next_sin = sin_y * cos_w + cos_y * sin_w
        cos_y = jnp.concatenate([cos_y, next_cos], axis=0)
        sin_y = jnp.concatenate([sin_y, next_sin], axis=0)
        sin_w, cos_w = 2.0 * sin_w * cos_w, 1.0 - 2.0 * sin_w * sin_w
        for start in range(0, half, 16):
            if start:
                cos_y, sin_y = cos_y * cos_w - sin_y * sin_w, sin_y * cos_w + cos_y * sin_w
            for value, ref in ((cos_y, cos_ref), (sin_y, sin_ref)):
                top = value.astype(jnp.bfloat16)
                ref[start : start + 16, cut] = top
                ref[half + start : half + start + 16, cut] = (value - top.astype(jnp.float32)).astype(jnp.bfloat16)


def block_source(block, each):
    count_x, count_y = lax.axis_size("gx"), lax.axis_size("gy")
    group = group_of("gx")
    place_x, place_y = lax.axis_index("gx"), lax.axis_index("gy")
    rest, within = block // each, block % each
    rest, far_y = rest // (count_y // 2), rest % (count_y // 2)
    rest, near_x = rest // group, rest % group
    core, far_x = rest // (count_x // group), rest % (count_x // group)
    owner_x = (far_x ^ (place_x // group)) * group + (place_x + near_x) % group
    owner_y = (far_y ^ (place_y // 2)) * 2 + (core ^ (place_y % 2))
    return (owner_x * count_y + owner_y) * each + within


def tables(waves, rows, width, scale):
    count = waves.shape[1]
    owned = count // (lax.axis_size("gx") * lax.axis_size("gy"))
    table = jax.ShapeDtypeStruct((width, count), jnp.bfloat16)
    return pl.pallas_call(
        partial(table_body, rows=rows, width=width, scale=scale, owned=owned),
        out_shape=(table, table, jax.ShapeDtypeStruct((32, count), jnp.float32)),
        scratch_shapes=[pltpu.VMEM((2, count // TABLE_CHUNK, TABLE_CHUNK), jnp.float32)],
        compiler_params=VMEM,
        cost_estimate=pl.CostEstimate(flops=40 * width * count, bytes_accessed=4 * width * count, transcendentals=0),
        name="tables",
    )(waves)


def project_body(even_ref, odd_ref, cos_ref, sin_ref, phase_ref, inner_ref, out_ref, *, start, pairs):
    chunk = 512
    for at in range(0, out_ref.shape[1], chunk):
        cut, to = slice(start + at, start + at + chunk), slice(at, at + chunk)
        real, imag = project_chunk((even_ref, odd_ref), cos_ref, sin_ref, phase_ref, cut, pairs)
        out_ref[0:8, to] = real + inner_ref[0:8, cut]
        out_ref[8:16, to] = imag + inner_ref[8:16, cut]


def project(planes, cos_y, sin_y, phases, inner, rows, start, count):
    width = cos_y.shape[0]
    return pl.pallas_call(
        partial(project_body, start=start, pairs=edge_pairs(rows)),
        out_shape=jax.ShapeDtypeStruct((16, count), jnp.float32),
        compiler_params=VMEM,
        cost_estimate=pl.CostEstimate(
            flops=8 * planes[0].shape[0] * width * count, bytes_accessed=4 * width * count, transcendentals=0
        ),
        name="project",
    )(*planes, cos_y, sin_y, phases, inner)


def swap(array, axis, mask):
    return lax.ppermute(array, axis, [(i, i ^ mask) for i in range(lax.axis_size(axis))])


def swap_other(array, axis):
    pairs = [(i, ((i + 1) ^ 1) - 1) for i in range(1, lax.axis_size(axis) - 1)]
    return lax.ppermute(array, axis, pairs)


def group_of(axis):
    return min(lax.axis_size(axis), 4)


def own_first(directions):
    count_x, count_y = lax.axis_size("gx"), lax.axis_size("gy")
    group = group_of("gx")
    waves = directions.T.reshape(2, count_x // group, group, count_y // 2, 2, -1)
    place_x, place_y = lax.axis_index("gx"), lax.axis_index("gy")
    waves = jnp.where(place_y % 2 == 1, jnp.flip(waves, 4), waves)
    waves = lax.dynamic_slice_in_dim(jnp.concatenate([waves, waves], axis=2), place_x % group, group, axis=2)
    waves = exclusive(waves, 1, place_x // group)
    waves = exclusive(waves, 3, place_y // 2)
    return waves.transpose(0, 4, 1, 2, 3, 5).reshape(2, directions.shape[0])


def exclusive(array, axis, place):
    size = array.shape[axis]
    bit = 1
    while bit < size:
        pieces = jnp.split(array, size // bit, axis)
        turned = jnp.concatenate([pieces[i ^ 1] for i in range(len(pieces))], axis)
        array = jnp.where(place & bit, turned, array)
        bit = 2 * bit
    return array


def halve(far, axis, mask):
    half = far.shape[1] // 2
    return far[:, :half] + swap(far[:, half:], axis, mask)


def halve_all(far, axis, low, size):
    mask = size // 2
    while mask >= 1:
        far = halve(far, axis, mask * low)
        mask = mask // 2
    return far


def scatter_group(far, axis):
    count, group = lax.axis_size(axis), group_of(axis)
    part = far.shape[1] // group
    total = far[:, :part]
    got = []
    for step in sorted(range(1, group), key=lambda step: (step != group // 2, step)):
        pairs = [(i, i // group * group + (i + step) % group) for i in range(count)]
        got.append(lax.ppermute(far[:, step * part : (step + 1) * part], axis, pairs))
    for array in got:
        total = total + array
    return total


def local(e_field, h_field, pol_now, pol_old, eps_inf, materials, surface, poles, directions):
    _, _, rows, width = e_field.shape
    scale = 1.0 / math.sqrt(rows * lax.axis_size("gx") * width * lax.axis_size("gy"))
    owned = directions.shape[0] // (lax.axis_size("gx") * lax.axis_size("gy"))
    waves = directions.T if owned % TABLE_CHUNK == 0 else own_first(directions)
    message, near, late, factors, e_field, h_field, waves = prepare(
        e_field, h_field, pol_now, pol_old, eps_inf, materials, poles, waves
    )
    one = swap(message, "gy", 1)
    two = swap_other(message, "gy")
    cos_y, sin_y, phases = tables(waves, rows, width, scale)
    own_one, own_two, h1, e1 = first_step(e_field, h_field, near, factors, one, two, phases)
    x_one = swap(own_one, "gx", 1)
    x_two = swap_other(own_two, "gx")
    inner = inside(h1, e1, late, factors, surface, cos_y, sin_y, phases)
    e_new, h_new, *planes = second_step(h1, e1, late, factors, surface, own_one, own_two, x_one, x_two)
    half = directions.shape[0] // 2
    far = project(planes, cos_y, sin_y, phases, inner, rows, half, half)
    arrived = swap(far, "gy", 1)
    far = project(planes, cos_y, sin_y, phases, inner, rows, 0, half) + arrived
    far = halve_all(far, "gx", group_of("gx"), lax.axis_size("gx") // group_of("gx"))
    far = scatter_group(far, "gx")
    far = halve_all(far, "gy", 2, lax.axis_size("gy") // 2)
    return e_new, h_new, far.T


def solution(mesh):
    field = P("design", None, "gx", "gy")
    cell = P("design", "gx", "gy")
    return jax.shard_map(
        local,
        mesh=mesh,
        in_specs=(field, field, field, field, cell, cell, cell, P(), P()),
        out_specs=(field, field, P(("gx", "gy"), "design")),
        check_vma=False,
    )
```
